512 devices in a mesh: segment: 4 (over z_lo), tm: 32 (over z_hi, y, core), dp: 4 (over x).
Axes of the slice: x: 4, y: 4, z: 16 (z_hi: 4, z_lo: 4; z = z_hi * 4 + z_lo), core: 2. Of those that a mesh axis runs over, the one named last changes fastest.
Arguments:
- features: bfloat16 [8, 128, 3, 8, 128], P('dp', 'tm'), may hold values from -6 to 6
- score_cot: float32 [8, 128, 3, 8], P('dp', 'tm'), may hold values from -6 to 6
- clip_frames: int32 [8], P('dp'), may hold values from 1 to 128, 768 in all
- conv_weights: bfloat16 [4, 2, 3456, 128], P('segment'), may hold values from -0.109375 to 0.109375
- norm_gains: float32 [4, 128], P('segment'), may hold values from 0.1 to 1.9
- score_head: float32 [128], replicated, may hold values from -0.5 to 0.5
Outputs:
- section_outputs: bfloat16 [4, 8, 128, 3, 8, 128], P('segment', 'dp', 'tm')
- weight_grads: bfloat16 [4, 2, 3456, 128], P('segment')
- section_input_grads: bfloat16 [4, 8, 128, 3, 8, 128], P('segment', 'dp', 'tm')
The draws below stay inside these ranges and needn't reach their ends.
Inputs may be any that keep to these rules, and one draw needn't show every extreme that they name: `clip_frames`: the longest clip has exactly 128 frames; the entries sum to 768.
All inputs are finite; a program needn't handle non-finite values. No bound on the sum of `clip_frames` on one device may be relied on, other than what follows from the above.
Results may differ from the reference program's by a relative error of at most 0.017.
Values may be sent and summed in bfloat16 or wider, within the bound.
A program may use at most 64 MiB of HBM per device.

```python
import math
import jax
import jax.numpy as jnp
import numpy as np
from jax import lax

C = 128
TILE_H = 3
TILE_W = 8
SEGMENTS = 4
BATCH = 8
FRAMES = 128


def steps_of(own_key, shape, cuts, low, high):
    loudness, own = 1.0, jax.random.fold_in(own_key, 6)
    for dim, shards_of in cuts:
        heights = jnp.exp(jax.random.uniform(jax.random.fold_in(own, dim), (shards_of,), jnp.float32, low / len(cuts), high / len(cuts)))
        loudness = loudness * jnp.repeat(heights, shape[dim] // shards_of).reshape([-1 if axis == dim else 1 for axis in range(len(shape))])
    return loudness


def profile(amount, total, bound, slope):
    portions = [(1 << 20) // math.isqrt(rank ** slope) + 1 for rank in range(2, amount + 1)]
    spare, holding = total - bound - (amount - 1), [1] * (amount - 1)
    while spare > 0:
        candidates = [i for i in range(amount - 1) if holding[i] < bound]
        whole, left = sum([portions[i] for i in candidates]), spare
        for i in candidates:
            extra = min(bound - holding[i], max(1, left * portions[i] // whole), spare)
            holding[i] = holding[i] + extra
            spare = spare - extra
    return np.array([bound] + holding)


def ragged_sizes(rng, number_of, total, reach, lean):
    if number_of == 2:
        one = jax.random.randint(rng, (), max(1, total - reach), min(reach, total - 1) + 1)
        return jnp.stack([one, total - one])
    sizes = jnp.asarray(profile(number_of, total, reach, lean), jnp.int32)
    pairs = (number_of - 1) // 2
    giver, receiver = sizes[1:1 + 2 * pairs:2], sizes[2:2 + 2 * pairs:2]
    margin = jnp.minimum(giver - 1, reach - receiver)
    passed = jax.random.randint(jax.random.fold_in(rng, 1), (pairs,), 0, 1 << 20) % (margin + 1)
    sizes = sizes.at[1:1 + 2 * pairs:2].set(giver - passed).at[2:2 + 2 * pairs:2].set(receiver + passed)
    return sizes[jax.random.permutation(jax.random.fold_in(rng, 2), number_of)]


def scatter_about(key, extent, width, reach, split=(), held_as=jnp.bfloat16):
    values = width * jax.random.normal(key, extent, jnp.float32)
    if split:
        values = values * steps_of(key, extent, split, -0.22, 0.18)
    return jnp.clip(values, -reach, reach).astype(held_as)


def setup_inputs(seed: int = 0) -> dict:
    keys = jax.random.split(jax.random.key(seed), 7)
    features = scatter_about(keys[0], (BATCH, FRAMES, TILE_H, TILE_W, C), 1.0, 6.0, ((0, 4), (1, 32)))
    score_cot = scatter_about(keys[1], (BATCH, FRAMES, TILE_H, TILE_W), 1.0, 6.0, ((0, 4), (1, 32)), jnp.float32)
    clip_frames = ragged_sizes(keys[2], BATCH, BATCH * FRAMES * 3 // 4, FRAMES, 0).astype(jnp.int32)
    conv_weights = scatter_about(keys[3], (SEGMENTS, 2, 27 * C, C), (27 * C) ** -0.5, 0.109375, ((0, 4),))
    norm_gains = jnp.clip(1.0 + 0.18 * jax.random.normal(keys[4], (SEGMENTS, C), jnp.float32), 0.1, 1.9)
    score_head = scatter_about(keys[5], (C,), C ** -0.5, 0.5, (), jnp.float32)
    return {"features": features, "score_cot": score_cot, "clip_frames": clip_frames, "conv_weights": conv_weights, "norm_gains": norm_gains, "score_head": score_head}


norm_eps = 1e-06

def patches(extended, frames):
    height = extended.shape[1]
    breadth = extended.shape[2]
    padded = jnp.pad(extended, ((0, 0), (1, 1), (1, 1), (0, 0)))
    pieces = []
    for tap_time in range(3):
        for tap_row in range(3):
            for tap_col in range(3):
                pieces.append(padded[tap_time:tap_time + frames, tap_row:tap_row + height, tap_col:tap_col + breadth])
    return jnp.concatenate(pieces, axis=-1).reshape(frames * height * breadth, -1)

def convolve(extended, kernel, frames):
    columns = patches(extended, frames).astype(jnp.float32)
    result = jnp.dot(columns, kernel.astype(jnp.float32), precision=lax.Precision.HIGHEST)
    return result.reshape(frames, extended.shape[1], extended.shape[2], kernel.shape[1])

def transpose_conv(cotangent, flipped):
    frames = cotangent.shape[0]
    widened = jnp.pad(cotangent, ((2, 2), (0, 0), (0, 0), (0, 0)))
    return convolve(widened, flipped, frames + 2)

def kernel_grad(extended, cotangent):
    frames = cotangent.shape[0]
    columns = patches(extended, frames).astype(jnp.float32)
    flat_cot = cotangent.reshape(-1, cotangent.shape[-1]).astype(jnp.float32)
    return lax.dot_general(columns, flat_cot, (((0,), (0,)), ((), ())), precision=lax.Precision.HIGHEST)

def flip_kernel(kernel):
    channels = kernel.shape[1]
    shaped = kernel.reshape(3, 3, 3, channels, channels)
    return jnp.transpose(shaped[::-1, ::-1, ::-1], (0, 1, 2, 4, 3)).reshape(27 * channels, channels)

def normalize(values, norm_gain):
    wide_values = values.astype(jnp.float32)
    inv_root = lax.rsqrt(lax.optimization_barrier(jnp.mean(wide_values * wide_values, axis=-1, keepdims=True)) + norm_eps)
    return (wide_values * inv_root * norm_gain).astype(jnp.bfloat16)

def norm_back(values, norm_gain, normed_cot):
    wide_values = values.astype(jnp.float32)
    inv_root = lax.rsqrt(lax.optimization_barrier(jnp.mean(wide_values * wide_values, axis=-1, keepdims=True)) + norm_eps)
    weighted = normed_cot * norm_gain
    inner = lax.optimization_barrier(jnp.mean(weighted * wide_values, axis=-1, keepdims=True))
    return inv_root * weighted - wide_values * inv_root * inv_root * inv_root * inner

def silu_slope(pre_act):
    sig_value = jax.nn.sigmoid(pre_act)
    return sig_value * (1.0 + pre_act * (1.0 - sig_value))

def reference(features, score_cot, clip_frames, conv_weights, norm_gains, score_head):
    frame_ids = jnp.arange(FRAMES, dtype=jnp.int32)
    valid_frames = (frame_ids[None, :] < clip_frames[:, None]).astype(jnp.float32)
    seed_grads = ((score_cot * valid_frames[:, :, None, None])[..., None] * score_head).astype(jnp.bfloat16)
    flip_pairs = [(flip_kernel(conv_weights[segment_index, 0]), flip_kernel(conv_weights[segment_index, 1])) for segment_index in range(SEGMENTS)]

    def one_clip(grad_total, clip_pair):
        clip_in, seed_grad = clip_pair
        current = clip_in
        saved_list = []
        block_outputs = []
        for segment_index in range(SEGMENTS):
            normed = normalize(current, norm_gains[segment_index])
            normed_ext = jnp.concatenate([jnp.zeros_like(normed[:2]), normed], axis=0)
            pre_act = convolve(normed_ext, conv_weights[segment_index, 0], FRAMES)
            hidden = jax.nn.silu(pre_act).astype(jnp.bfloat16)
            hidden_ext = jnp.concatenate([jnp.zeros_like(hidden[:2]), hidden], axis=0)
            second = convolve(hidden_ext, conv_weights[segment_index, 1], FRAMES)
            block_out = (current.astype(jnp.float32) + second).astype(jnp.bfloat16)
            saved_list.append((current, normed_ext, pre_act, hidden_ext))
            block_outputs.append(block_out)
            current = block_out
        grad_out = seed_grad
        grad_list = []
        input_list = []
        for segment_index in reversed(range(SEGMENTS)):
            block_in, normed_ext, pre_act, hidden_ext = saved_list[segment_index]
            second_grad = kernel_grad(hidden_ext, grad_out)
            hidden_cot = transpose_conv(grad_out, flip_pairs[segment_index][1])[2:]
            pre_cot = (hidden_cot * silu_slope(pre_act)).astype(jnp.bfloat16)
            first_grad = kernel_grad(normed_ext, pre_cot)
            normed_cot = transpose_conv(pre_cot, flip_pairs[segment_index][0])[2:]
            grad_out = (grad_out.astype(jnp.float32) + norm_back(block_in, norm_gains[segment_index], normed_cot)).astype(jnp.bfloat16)
            grad_list.append(jnp.stack([first_grad, second_grad]))
            input_list.append(grad_out)
        clip_grads = jnp.stack(grad_list[::-1])
        return (grad_total + clip_grads, (jnp.stack(block_outputs), jnp.stack(input_list[::-1])))
    start_grads = jnp.zeros((SEGMENTS, 2, 27 * C, C), jnp.float32)
    grad_total, stacked = lax.scan(one_clip, start_grads, (features, seed_grads))
    outputs, input_grads = stacked
    section_outputs = jnp.transpose(outputs, (1, 0, 2, 3, 4, 5))
    section_input_grads = jnp.transpose(input_grads, (1, 0, 2, 3, 4, 5))
    return (section_outputs, grad_total.astype(jnp.bfloat16), section_input_grads)
```

```python
import functools

import jax
import jax.numpy as jnp
from jax import lax
from jax.experimental import pallas as pl
from jax.experimental.pallas import tpu as pltpu
from jax.sharding import PartitionSpec as P

norm_eps = 1e-06
FRAMES_HERE = 4
GROUP = 7
BAND = 32
BF, F32 = jnp.bfloat16, jnp.float32


def column_shifts(values):
    shape = values.shape
    flat = values.reshape(-1, 8, 128)
    column = lax.broadcasted_iota(jnp.int32, flat.shape, 1)
    before = jnp.where(column == 0, 0.0, pltpu.roll(flat, 1, 1))
    after = jnp.where(column == 7, 0.0, pltpu.roll(flat, 7, 1))
    return [before.reshape(shape), values, after.reshape(shape)]


def fill(patch_ref, values):
    frames = values.shape[0]
    for e, shifted in enumerate(column_shifts(values)):
        patch_ref[:frames, 1:4, :, e * 128 : (e + 1) * 128] = shifted.astype(BF)


def convolve(patch_ref, weight_ref, which, frames):
    total = None
    for a in range(3):
        for b in range(3):
            rows = patch_ref[a : a + frames, b : b + 3].reshape(frames * 48, 384)
            taps = weight_ref[which, (9 * a + 3 * b) * 128 : (9 * a + 3 * b + 3) * 128, :]
            part = jnp.dot(rows, taps, preferred_element_type=F32)
            total = part if total is None else total + part
    return total.reshape(frames, 3, 16, 128)


def kernel(
    S, T, Y, Z,
    feat_ref, score_ref, clip_ref, weight_hbm, gain_ref, head_ref,
    out_ref, grad_ref, back_ref,
    weight, flipped, xin, din, slope, patch8, patch6, vsend, vbuf, vt, upad, pcot, gsend, r1, s1, r2, zbuf,
    local_sem, send_sem, recv_sem,
):
    seg, t, x = lax.axis_index("segment"), lax.axis_index("tm"), lax.axis_index("dp")
    core = lax.rem(t, 2)
    y = lax.rem(t // 2, Y)
    z = t // (2 * Y)
    frames = FRAMES_HERE

    def time_of(z, y, core):
        return (z * Y + y) * 2 + core

    def to(seg_to, t_to, x_to):
        return {"segment": seg_to, "tm": t_to, "dp": x_to}

    def remote(source, target, send, recv, device):
        return pltpu.make_async_remote_copy(
            src_ref=source, dst_ref=target, send_sem=send_sem.at[send], recv_sem=recv_sem.at[recv],
            device_id=device, device_id_type=pl.DeviceIdType.MESH,
        )

    load = pltpu.make_async_copy(weight_hbm.at[0], weight, local_sem)
    load.start()

    patch8[:, 0] = jnp.zeros_like(patch8[:, 0])
    patch8[:, 4] = jnp.zeros_like(patch8[:, 4])
    patch6[:, 0] = jnp.zeros_like(patch6[:, 0])
    patch6[:, 4] = jnp.zeros_like(patch6[:, 4])
    upad[...] = jnp.zeros_like(upad)
    gsend[27] = jnp.zeros_like(gsend[27])
    has_before, has_after = t > 0, t < T - 1
    below, above = seg > 0, seg < S - 1
    before, after = jnp.maximum(t - 1, 0), jnp.minimum(t + 1, T - 1)
    lower, upper = jnp.maximum(seg - 1, 0), jnp.minimum(seg + 1, S - 1)

    @pl.when(jnp.logical_not(has_before))
    def _():
        xin[0:frames] = jnp.zeros_like(xin[0:frames])

    @pl.when(jnp.logical_not(has_after))
    def _():
        din[frames:] = jnp.zeros_like(din[frames:])
        slope[frames:] = jnp.zeros_like(slope[frames:])

    barrier = pltpu.get_barrier_semaphore()
    expected = 9
    for condition, device in (
        (has_before, to(seg, before, x)),
        (has_after, to(seg, after, x)),
        (above, to(upper, t, x)),
        (jnp.logical_and(above, has_after), to(upper, after, x)),
        (below, to(lower, t, x)),
        (jnp.logical_and(below, has_before), to(lower, before, x)),
    ):
        expected = expected + condition.astype(jnp.int32)

        @pl.when(condition)
        def _(device=device):
            pl.semaphore_signal(barrier, 1, device_id=device, device_id_type=pl.DeviceIdType.MESH)

    for step in range(1, 4):
        for device in (
            to(seg, t, lax.rem(x + step, 4)),
            to(seg, time_of(z, lax.rem(y + step, 4), core), x),
            to(seg, time_of(lax.rem(z + step, 4), y, core), x),
        ):
            pl.semaphore_signal(barrier, 1, device_id=device, device_id_type=pl.DeviceIdType.MESH)

    def own_features():
        return jnp.concatenate([feat_ref[0].astype(F32), feat_ref[1].astype(F32)], axis=2)

    @pl.when(seg == 0)
    def _():
        xin[frames:] = own_features().astype(BF)

    @pl.when(seg == S - 1)
    def _():
        eye = lax.broadcasted_iota(jnp.int32, (8, 8), 0) == lax.broadcasted_iota(jnp.int32, (8, 8), 1)
        head = head_ref[...]
        for f in range(frames):
            for i in range(3):
                halves = []
                for n in range(2):
                    line = score_ref[n, f, i : i + 1, :]
                    valid = jnp.where(t * frames + f < clip_ref[n], 1.0, 0.0)
                    stood = jnp.sum(jnp.where(eye, jnp.broadcast_to(line, (8, 8)), 0.0), axis=1, keepdims=True)
                    halves.append((stood * valid) * head)
                din[f, i] = jnp.concatenate(halves, axis=0).astype(BF)

    pl.semaphore_wait(barrier, expected)

    own_x = remote(xin.at[pl.ds(frames, frames)], xin.at[pl.ds(0, frames)], 0, 0, to(seg, after, x))
    own_d = remote(din.at[pl.ds(0, frames)], din.at[pl.ds(frames, frames)], 1, 1, to(seg, before, x))
    x_up = remote(out_ref, xin.at[pl.ds(frames, frames)], 2, 2, to(upper, t, x))
    x_up_after = remote(out_ref, xin.at[pl.ds(0, frames)], 23, 0, to(upper, after, x))
    d_down = remote(back_ref, din.at[pl.ds(0, frames)], 3, 3, to(lower, t, x))
    d_down_before = remote(back_ref, din.at[pl.ds(frames, frames)], 24, 1, to(lower, before, x))
    slope_back = remote(slope.at[pl.ds(0, 2)], slope.at[pl.ds(4, 2)], 4, 4, to(seg, before, x))
    partner = to(seg, t + 1 - 2 * core, x)
    v_swap = remote(vsend, vbuf.at[pl.ds(6 * core, 4)], 5, 5, partner)
    u_to_one = remote(din.at[pl.ds(0, 4)], upad.at[pl.ds(2, 4), pl.ds(1, 3)], 6, 6, partner)
    u_to_zero = remote(pcot, upad.at[pl.ds(8, 2), pl.ds(1, 3)], 6, 6, partner)

    @pl.when(jnp.logical_and(seg == 0, has_after))
    def _():
        own_x.start()

    @pl.when(jnp.logical_and(seg == S - 1, has_before))
    def _():
        own_d.start()

    load.wait()

    def flip_all():
        def one(i, carry):
            source = pl.multiple_of(i * 128, 128)
            target = pl.multiple_of((26 - i) * 128, 128)
            for which in range(2):
                tap = weight[which, pl.ds(source, 128), :].astype(F32)
                flipped[which, pl.ds(target, 128), :] = tap.T.astype(BF)
            return carry

        lax.fori_loop(0, 27, one, 0)

    @pl.when(below)
    def _():
        flip_all()

    @pl.when(below)
    def _():
        x_up.wait_recv()

    @pl.when(has_before)
    def _():
        x_up_after.wait_recv()

    gain = gain_ref[...]
    wide = xin[...].astype(F32)
    root = lax.rsqrt(jnp.mean(wide * wide, axis=-1, keepdims=True) + norm_eps)
    normed = (wide * root * gain).astype(BF).astype(F32)
    fill(patch8, normed)
    pre = convolve(patch8, weight, 0, 6)
    sig = 1.0 / (1.0 + jnp.exp(-pre))
    hidden = (pre * sig).astype(BF).astype(F32)
    slope[0:4] = (sig * (1.0 + pre * (1.0 - sig)))[2:6]

    @pl.when(has_before)
    def _():
        slope_back.start()

    fill(patch6, hidden)
    vsend[...] = jnp.where(core == 0, hidden[0:4], normed[4:8]).astype(BF)
    vbuf[pl.ds(4 * core, 6)] = jnp.where(core == 0, normed[2:8], hidden).astype(BF)
    v_swap.start()
    second = convolve(patch6, weight, 1, 4)
    out_ref[...] = (xin[4:8].astype(F32) + second).astype(BF)

    @pl.when(above)
    def _():
        x_up.start()

    @pl.when(jnp.logical_and(above, has_after))
    def _():
        x_up_after.start()

    def stand_up():
        v_swap.wait_recv()
        flat = vbuf[...].astype(F32)
        for e, shifted in enumerate(column_shifts(flat)):
            rows = jnp.concatenate([shifted.reshape(480, 128), jnp.zeros((32, 128), F32)], axis=0)
            vt[e * 128 : (e + 1) * 128, :] = rows.T.astype(BF)

    @pl.when(seg == 0)
    def _():
        flip_all()

    @pl.when(above)
    def _():
        stand_up()

    @pl.when(above)
    def _():
        d_down.wait_recv()

    @pl.when(core == 0)
    def _():
        u_to_one.start()

    @pl.when(core == 1)
    def _():
        upad[6:10, 1:4] = din[0:4]

    @pl.when(has_after)
    def _():
        d_down_before.wait_recv()

    fill(patch8, din[...].astype(F32))
    hidden_cot = convolve(patch8, flipped, 1, 6)

    @pl.when(has_after)
    def _():
        slope_back.wait_recv()

    pre_cot = (hidden_cot * slope[...]).astype(BF)

    @pl.when(core == 0)
    def _():
        upad[2:8, 1:4] = pre_cot

    @pl.when(core == 1)
    def _():
        pcot[...] = pre_cot[2:4]
        u_to_zero.start()

    fill(patch6, pre_cot.astype(F32))
    normed_cot = convolve(patch6, flipped, 0, 4)
    wide = xin[4:8].astype(F32)
    root = lax.rsqrt(jnp.mean(wide * wide, axis=-1, keepdims=True) + norm_eps)
    weighted = normed_cot * gain
    inner = jnp.mean(weighted * wide, axis=-1, keepdims=True)
    back_ref[...] = (din[0:4].astype(F32) + (root * weighted - wide * root * root * root * inner)).astype(BF)

    @pl.when(below)
    def _():
        d_down.start()

    @pl.when(jnp.logical_and(below, has_before))
    def _():
        d_down_before.start()

    @pl.when(seg == S - 1)
    def _():
        stand_up()

    first, other = jnp.where(core == 0, x, y), jnp.where(core == 0, y, x)

    def on_first(step):
        turned = lax.rem(first + step, 4)
        return to(seg, time_of(z, jnp.where(core == 0, y, turned), core), jnp.where(core == 0, turned, x))

    def on_other(step):
        turned = lax.rem(other + step, 4)
        return to(seg, time_of(z, jnp.where(core == 0, turned, y), core), jnp.where(core == 0, x, turned))

    def group_at(step):
        return pl.ds(lax.rem(first + step, 4) * GROUP, GROUP)

    def band_at(step):
        return pl.ds(pl.multiple_of(lax.rem(other + step, 4) * BAND, BAND), BAND)

    @pl.when(core == 0)
    def _():
        u_to_zero.wait_recv()

    @pl.when(core == 1)
    def _():
        u_to_one.wait_recv()

    for a in range(3):
        for b in range(3):
            rows = upad[2 - a : 12 - a, 2 - b : 5 - b].reshape(480, 128)
            rows = jnp.concatenate([rows, jnp.zeros((32, 128), BF)], axis=0)
            part = jnp.dot(vt[...], rows, preferred_element_type=F32)
            gsend[9 * a + 3 * b : 9 * a + 3 * b + 3] = part.astype(BF).reshape(3, 128, 128)

    round1 = [remote(gsend.at[group_at(k)], r1.at[k - 1], 7 + k, 7 + k, on_first(k)) for k in range(1, 4)]
    for copy in round1:
        copy.start()
    total = gsend[group_at(0)].astype(F32)
    for k in range(3):
        round1[k].wait_recv()
        total = total + r1[k].astype(F32)
    s1[...] = total.astype(BF)
    round2 = [remote(s1.at[:, band_at(k)], r2.at[k - 1], 10 + k, 10 + k, on_other(k)) for k in range(1, 4)]
    for copy in round2:
        copy.start()
    total = s1[:, band_at(0)].astype(F32)
    for k in range(3):
        round2[k].wait_recv()
        total = total + r2[k].astype(F32)
    zbuf[z] = total.astype(BF)
    round3 = [
        remote(zbuf.at[z], zbuf.at[z], 13 + k, 13 + k, to(seg, time_of(lax.rem(z + k, 4), y, core), x))
        for k in range(1, 4)
    ]
    for copy in round3:
        copy.start()
    for k in range(3):
        round3[k].wait_recv()
    total = zbuf[0].astype(F32) + zbuf[1].astype(F32) + zbuf[2].astype(F32) + zbuf[3].astype(F32)
    grad_ref[core, group_at(0), band_at(0)] = total.astype(BF)
    piece = grad_ref.at[core, group_at(0), band_at(0)]
    round4 = [remote(piece, piece, 16 + k, 16 + k, on_other(k)) for k in range(1, 4)]
    for copy in round4:
        copy.start()
    for copy in round4:
        copy.wait_recv()
    whole = grad_ref.at[core, group_at(0)]
    round5 = [remote(whole, whole, 19 + k, 19 + k, on_first(k)) for k in range(1, 4)]
    for copy in round5:
        copy.start()
    round6 = []
    for k in range(4):
        held = grad_ref.at[core, group_at((4 - k) % 4)]
        forward = remote(held, held, 25 + k, 23 + k, partner)
        if k > 0:
            round5[k - 1].wait_recv()
        forward.start()
        round6.append(forward)
    for copy in round6:
        copy.wait_recv()

    for copy in round1 + round2 + round3 + round4 + round5 + round6:
        copy.wait_send()
    v_swap.wait_send()

    @pl.when(core == 0)
    def _():
        u_to_one.wait_send()

    @pl.when(core == 1)
    def _():
        u_to_zero.wait_send()

    @pl.when(has_before)
    def _():
        slope_back.wait_send()

    @pl.when(jnp.logical_and(seg == 0, has_after))
    def _():
        own_x.wait_send()

    @pl.when(jnp.logical_and(seg == S - 1, has_before))
    def _():
        own_d.wait_send()

    @pl.when(above)
    def _():
        x_up.wait_send()

    @pl.when(jnp.logical_and(above, has_after))
    def _():
        x_up_after.wait_send()

    @pl.when(below)
    def _():
        d_down.wait_send()

    @pl.when(jnp.logical_and(below, has_before))
    def _():
        d_down_before.wait_send()


def solution(mesh):
    S, T = mesh.shape["segment"], mesh.shape["tm"]
    Y = 4
    Z = T // (2 * Y)
    vmem = pl.BlockSpec(memory_space=pltpu.VMEM)
    cells = (FRAMES_HERE, 3, 16, 128)

    def body(features, score_cot, clip_frames, conv_weights, norm_gains, score_head):
        out, grad, back = pl.pallas_call(
            functools.partial(kernel, S, T, Y, Z),
            out_shape=(
                jax.ShapeDtypeStruct(cells, BF),
                jax.ShapeDtypeStruct((2, 28, 128, 128), BF),
                jax.ShapeDtypeStruct(cells, BF),
            ),
            in_specs=[
                vmem, vmem, pl.BlockSpec(memory_space=pltpu.SMEM), pl.BlockSpec(memory_space=pl.ANY), vmem, vmem,
            ],
            out_specs=(vmem, vmem, vmem),
            scratch_shapes=[
                pltpu.VMEM((2, 3456, 128), BF),
                pltpu.VMEM((2, 3456, 128), BF),
                pltpu.VMEM((8, 3, 16, 128), BF),
                pltpu.VMEM((8, 3, 16, 128), BF),
                pltpu.VMEM((6, 3, 16, 128), F32),
                pltpu.VMEM((8, 5, 16, 384), BF),
                pltpu.VMEM((6, 5, 16, 384), BF),
                pltpu.VMEM((4, 3, 16, 128), BF),
                pltpu.VMEM((10, 3, 16, 128), BF),
                pltpu.VMEM((384, 512), BF),
                pltpu.VMEM((12, 5, 16, 128), BF),
                pltpu.VMEM((2, 3, 16, 128), BF),
                pltpu.VMEM((28, 128, 128), BF),
                pltpu.VMEM((3, GROUP, 128, 128), BF),
                pltpu.VMEM((GROUP, 128, 128), BF),
                pltpu.VMEM((3, GROUP, BAND, 128), BF),
                pltpu.VMEM((4, GROUP, BAND, 128), BF),
                pltpu.SemaphoreType.DMA,
                pltpu.SemaphoreType.DMA((29,)),
                pltpu.SemaphoreType.DMA((27,)),
            ],
            compiler_params=pltpu.CompilerParams(
                collective_id=0, has_side_effects=True, vmem_limit_bytes=40 * 1024 * 1024
            ),
            cost_estimate=pl.CostEstimate(flops=10**9, bytes_accessed=6 * 10**6, transcendentals=10**5),
        )(features, score_cot, clip_frames, conv_weights, norm_gains, score_head.reshape(1, 128))

        def split_clips(cells):
            return jnp.transpose(cells.reshape(FRAMES_HERE, 3, 2, 8, 128), (2, 0, 1, 3, 4))[None]

        return split_clips(out), grad[:, :27].reshape(1, 2, 3456, 128), split_clips(back)

    return jax.shard_map(
        body,
        mesh=mesh,
        in_specs=(
            P("dp", "tm", None, None, None),
            P("dp", "tm", None, None),
            P("dp"),
            P("segment", None, None, None),
            P("segment", None),
            P(),
        ),
        out_specs=(
            P("segment", "dp", "tm", None, None, None),
            P("segment", None, None, None),
            P("segment", "dp", "tm", None, None, None),
        ),
        check_vma=False,
    )
```

```python
import functools

import jax
import jax.numpy as jnp
from jax import lax
from jax.experimental import pallas as pl
from jax.experimental.pallas import tpu as pltpu
from jax.sharding import PartitionSpec as P

norm_eps = 1e-06
FRAMES_HERE = 4
GROUP = 7
BAND = 16
SENDS = 112
BF, F32 = jnp.bfloat16, jnp.float32


def column_shifts(values):
    shape = values.shape
    flat = values.reshape(-1, 8, 128)
    column = lax.broadcasted_iota(jnp.int32, flat.shape, 1)
    before = jnp.where(column == 0, 0.0, pltpu.roll(flat, 1, 1))
    after = jnp.where(column == 7, 0.0, pltpu.roll(flat, 7, 1))
    return [before.reshape(shape), values, after.reshape(shape)]


def fill(patch_ref, values):
    frames = values.shape[0]
    for e, shifted in enumerate(column_shifts(values)):
        patch_ref[:frames, 1:4, :, e * 128 : (e + 1) * 128] = shifted.astype(BF)


def convolve(patch_ref, weight_ref, which, frames, at=0):
    total = None
    for a in range(3):
        for b in range(3):
            rows = patch_ref[at + a : at + a + frames, b : b + 3].reshape(frames * 48, 384)
            taps = weight_ref[which, (9 * a + 3 * b) * 128 : (9 * a + 3 * b + 3) * 128, :]
            part = jnp.dot(rows, taps, preferred_element_type=F32)
            total = part if total is None else total + part
    return total.reshape(frames, 3, 16, 128)


def kernel(
    S, T, Y, Z,
    feat_hbm, score_hbm, clip_hbm, weight_hbm, gain_hbm, head_hbm,
    out_ref, grad_ref, back_ref,
    feat_ref, score_ref, clip_ref, gain_ref, head_ref, own, weight, flipped, xin, din, slope, patch8, patch6, vsend, vbuf, vt, upad, pcot, gsend, r1, s1, r2, zbuf,
    local_sem, send_sem, recv_sem, ready,
):
    seg, t, x = lax.axis_index("segment"), lax.axis_index("tm"), lax.axis_index("dp")
    core = lax.rem(t, 2)
    y = lax.rem(t // 2, Y)
    z = t // (2 * Y)
    frames = FRAMES_HERE

    def time_of(z, y, core):
        return (z * Y + y) * 2 + core

    def to(seg_to, t_to, x_to):
        return {"segment": seg_to, "tm": t_to, "dp": x_to}

    def remote(source, target, send, recv, device):
        return pltpu.make_async_remote_copy(
            src_ref=source, dst_ref=target, send_sem=send_sem.at[send], recv_sem=recv_sem.at[recv],
            device_id=device, device_id_type=pl.DeviceIdType.MESH,
        )

    loads = [
        pltpu.make_async_copy(source, target, local_sem.at[i])
        for i, (source, target) in enumerate((
            (feat_hbm, feat_ref), (gain_hbm, gain_ref), (weight_hbm.at[0], weight),
            (score_hbm, score_ref), (clip_hbm, clip_ref), (head_hbm, head_ref),
        ))
    ]
    for load in loads:
        load.start()

    patch8[:, 0] = jnp.zeros_like(patch8[:, 0])
    patch8[:, 4] = jnp.zeros_like(patch8[:, 4])
    patch6[:, 0] = jnp.zeros_like(patch6[:, 0])
    patch6[:, 4] = jnp.zeros_like(patch6[:, 4])
    upad[...] = jnp.zeros_like(upad)
    gsend[27] = jnp.zeros_like(gsend[27])
    has_before, has_after = t > 0, t < T - 1
    seam_after = jnp.logical_and(has_after, lax.rem(t, 2 * Y) == 2 * Y - 1)
    seam_before = jnp.logical_and(has_before, lax.rem(t, 2 * Y) == 0)
    bridge_after = jnp.logical_and(seg == S - 1, seam_after)
    bridge_before = jnp.logical_and(seg == 0, seam_before)
    below, above = seg > 0, seg < S - 1
    before, after = jnp.maximum(t - 1, 0), jnp.minimum(t + 1, T - 1)
    lower, upper = jnp.maximum(seg - 1, 0), jnp.minimum(seg + 1, S - 1)

    @pl.when(jnp.logical_not(has_before))
    def _():
        xin[0:frames] = jnp.zeros_like(xin[0:frames])

    @pl.when(jnp.logical_not(has_after))
    def _():
        din[frames:] = jnp.zeros_like(din[frames:])
        slope[frames:] = jnp.zeros_like(slope[frames:])

    barrier = pltpu.get_barrier_semaphore()
    expected = 8
    for condition, device in (
        (has_before, to(seg, before, x)),
        (has_after, to(seg, after, x)),
        (above, to(upper, t, x)),
        (jnp.logical_and(above, has_after), to(upper, after, x)),
        (below, to(lower, t, x)),
        (jnp.logical_and(below, has_before), to(lower, before, x)),
        (bridge_after, to(0, after, x)),
        (bridge_before, to(S - 1, before, x)),
    ):
        expected = expected + condition.astype(jnp.int32)

        @pl.when(condition)
        def _(device=device):
            pl.semaphore_signal(barrier, 1, device_id=device, device_id_type=pl.DeviceIdType.MESH)

    for device in [
        *(to(seg, t, lax.rem(x + step, 4)) for step in range(1, 4)),
        *(to(seg, time_of(z, lax.rem(y + step, 4), core), x) for step in range(1, 4)),
        *(to(seg, time_of(lax.rem(z + step, 4), y, core), x) for step in (1, 3)),
    ]:
        pl.semaphore_signal(barrier, 1, device_id=device, device_id_type=pl.DeviceIdType.MESH)

    def put_features(target):
        target[...] = jnp.concatenate([feat_ref[0].astype(F32), feat_ref[1].astype(F32)], axis=2).astype(BF)

    def put_seeds(target):
        eye = lax.broadcasted_iota(jnp.int32, (8, 8), 0) == lax.broadcasted_iota(jnp.int32, (8, 8), 1)
        head = head_ref[...]
        for f in range(frames):
            for i in range(3):
                halves = []
                for n in range(2):
                    line = score_ref[n, i, f : f + 1, :]
                    valid = jnp.where(t * frames + f < clip_ref[n], 1.0, 0.0)
                    stood = jnp.sum(jnp.where(eye, jnp.broadcast_to(line, (8, 8)), 0.0), axis=1, keepdims=True)
                    halves.append((stood * valid) * head)
                target[f, i] = jnp.concatenate(halves, axis=0).astype(BF)

    for load in loads:
        load.wait()

    @pl.when(seg == 0)
    def _():
        put_features(xin.at[pl.ds(frames, frames)])

    @pl.when(seg == S - 1)
    def _():
        put_features(own)
        put_seeds(din.at[pl.ds(0, frames)])

    pl.semaphore_wait(barrier, expected)
    pl.semaphore_signal(
        ready, 1, device_id=to(seg, time_of(lax.rem(z + 3, 4), y, core), x), device_id_type=pl.DeviceIdType.MESH
    )

    own_x = remote(xin.at[pl.ds(frames, frames)], xin.at[pl.ds(0, frames)], 0, 0, to(seg, after, x))
    own_d = remote(din.at[pl.ds(0, frames)], din.at[pl.ds(frames, frames)], 1, 1, to(seg, before, x))
    seam_x = remote(own, xin.at[pl.ds(0, frames)], 0, 0, to(0, after, x))
    seam_d = remote(own, din.at[pl.ds(frames, frames)], 1, 1, to(S - 1, before, x))
    x_up, d_down = [], []
    for h in range(2):
        here, later = pl.ds(2 * h, 2), pl.ds(frames + 2 * h, 2)
        x_up.append((
            remote(out_ref.at[here], xin.at[later], 2 + h, 2 + h, to(upper, t, x)),
            remote(out_ref.at[here], xin.at[here], 4 + h, 4 + h, to(upper, after, x)),
        ))
        d_down.append((
            remote(back_ref.at[here], din.at[here], 6 + h, 6 + h, to(lower, t, x)),
            remote(back_ref.at[here], din.at[later], 8 + h, 8 + h, to(lower, before, x)),
        ))
    slope_back = remote(slope.at[pl.ds(0, 2)], slope.at[pl.ds(4, 2)], 10, 10, to(seg, before, x))
    partner = to(seg, t + 1 - 2 * core, x)
    v_swap = remote(vsend, vbuf.at[pl.ds(6 * core, 4)], 11, 11, partner)
    u_to_one = remote(din.at[pl.ds(0, 4)], upad.at[pl.ds(2, 4), pl.ds(1, 3)], 12, 12, partner)
    u_to_zero = remote(pcot, upad.at[pl.ds(8, 2), pl.ds(1, 3)], 12, 12, partner)
    plain_x = jnp.logical_and(seg == 0, jnp.logical_and(has_after, jnp.logical_not(seam_after)))
    plain_d = jnp.logical_and(seg == S - 1, jnp.logical_and(has_before, jnp.logical_not(seam_before)))

    @pl.when(plain_x)
    def _():
        own_x.start()

    @pl.when(bridge_after)
    def _():
        seam_x.start()

    @pl.when(plain_d)
    def _():
        own_d.start()

    def flip_all():
        def one(i, carry):
            source = pl.multiple_of(i * 128, 128)
            target = pl.multiple_of((26 - i) * 128, 128)
            for which in range(2):
                tap = weight[which, pl.ds(source, 128), :].astype(F32)
                flipped[which, pl.ds(target, 128), :] = tap.T.astype(BF)
            return carry

        lax.fori_loop(0, 27, one, 0)

    @pl.when(below)
    def _():
        flip_all()

    @pl.when(below)
    def _():
        for straight, _ in x_up:
            straight.wait_recv()

    @pl.when(jnp.logical_and(below, has_before))
    def _():
        for _, across in x_up:
            across.wait_recv()

    @pl.when(jnp.logical_and(seg == 0, has_before))
    def _():
        own_x.wait_recv()

    gain = gain_ref[...]
    wide = xin[...].astype(F32)
    root = lax.rsqrt(jnp.mean(wide * wide, axis=-1, keepdims=True) + norm_eps)
    normed = (wide * root * gain).astype(BF).astype(F32)
    fill(patch8, normed)
    pre = convolve(patch8, weight, 0, 6)
    sig = 1.0 / (1.0 + jnp.exp(-pre))
    hidden = (pre * sig).astype(BF).astype(F32)
    slope[0:4] = (sig * (1.0 + pre * (1.0 - sig)))[2:6]

    @pl.when(has_before)
    def _():
        slope_back.start()

    fill(patch6, hidden)
    vsend[...] = jnp.where(core == 0, hidden[0:4], normed[4:8]).astype(BF)
    vbuf[pl.ds(4 * core, 6)] = jnp.where(core == 0, normed[2:8], hidden).astype(BF)
    v_swap.start()
    for h in range(2):
        rows = slice(2 * h, 2 * h + 2)
        second = convolve(patch6, weight, 1, 2, 2 * h)
        out_ref[rows] = (xin[4 + 2 * h : 6 + 2 * h].astype(F32) + second).astype(BF)

        @pl.when(jnp.logical_and(above, has_after))
        def _(h=h):
            x_up[h][1].start()

        @pl.when(above)
        def _(h=h):
            x_up[h][0].start()

    def stand_up():
        v_swap.wait_recv()
        flat = vbuf[...].astype(F32)
        for e, shifted in enumerate(column_shifts(flat)):
            rows = jnp.concatenate([shifted.reshape(480, 128), jnp.zeros((32, 128), F32)], axis=0)
            vt[e * 128 : (e + 1) * 128, :] = rows.T.astype(BF)

    @pl.when(bridge_before)
    def _():
        put_seeds(own)
        seam_d.start()

    @pl.when(seg == 0)
    def _():
        flip_all()

    @pl.when(above)
    def _():
        stand_up()

    @pl.when(above)
    def _():
        for straight, _ in d_down:
            straight.wait_recv()

    @pl.when(core == 0)
    def _():
        u_to_one.start()

    @pl.when(core == 1)
    def _():
        upad[6:10, 1:4] = din[0:4]

    @pl.when(jnp.logical_and(above, has_after))
    def _():
        for _, across in d_down:
            across.wait_recv()

    @pl.when(jnp.logical_and(seg == S - 1, has_after))
    def _():
        own_d.wait_recv()

    fill(patch8, din[...].astype(F32))
    hidden_cot = convolve(patch8, flipped, 1, 6)

    @pl.when(has_after)
    def _():
        slope_back.wait_recv()

    pre_cot = (hidden_cot * slope[...]).astype(BF)

    @pl.when(core == 0)
    def _():
        upad[2:8, 1:4] = pre_cot

    @pl.when(core == 1)
    def _():
        pcot[...] = pre_cot[2:4]
        u_to_zero.start()

    fill(patch6, pre_cot.astype(F32))
    for h in range(2):
        rows = slice(2 * h, 2 * h + 2)
        normed_cot = convolve(patch6, flipped, 0, 2, 2 * h)
        wide = xin[4 + 2 * h : 6 + 2 * h].astype(F32)
        root = lax.rsqrt(jnp.mean(wide * wide, axis=-1, keepdims=True) + norm_eps)
        weighted = normed_cot * gain
        inner = jnp.mean(weighted * wide, axis=-1, keepdims=True)
        back_ref[rows] = (din[rows].astype(F32) + (root * weighted - wide * root * root * root * inner)).astype(BF)

        @pl.when(jnp.logical_and(below, has_before))
        def _(h=h):
            d_down[h][1].start()

        @pl.when(below)
        def _(h=h):
            d_down[h][0].start()

    @pl.when(seg == S - 1)
    def _():
        stand_up()

    def on_x(step):
        return to(seg, t, lax.rem(x + step, 4))

    def on_y(step):
        return to(seg, time_of(z, lax.rem(y + step, 4), core), x)

    first, other = (x, y), (y, x)
    on_first, on_other = (on_x, on_y), (on_y, on_x)

    def group_at(h, step):
        return pl.ds(lax.rem(first[h] + step, 4) * GROUP, GROUP)

    def band_at(h, step):
        return pl.ds(pl.multiple_of(64 * h + lax.rem(other[h] + step, 4) * BAND, BAND), BAND)

    def piece(h, j, k):
        return grad_ref.at[core, group_at(h, j), band_at(h, k)]

    @pl.when(core == 0)
    def _():
        u_to_zero.wait_recv()

    @pl.when(core == 1)
    def _():
        u_to_one.wait_recv()

    for a in range(3):
        for b in range(3):
            rows = upad[2 - a : 12 - a, 2 - b : 5 - b].reshape(480, 128)
            rows = jnp.concatenate([rows, jnp.zeros((32, 128), BF)], axis=0)
            part = jnp.dot(vt[...], rows, preferred_element_type=F32)
            gsend[9 * a + 3 * b : 9 * a + 3 * b + 3] = part.astype(BF).reshape(3, 128, 128)

    started = []

    def send(source, target, device):
        index = len(started)
        copy = remote(source, target, 13 + index, 13 + index, device)
        copy.start()
        started.append(copy)
        return copy

    scattered = {}
    for k in (1, 2, 3, 0):
        for j in range(1, 4):
            for h in range(2):
                scattered[h, j, k] = send(gsend.at[group_at(h, j), band_at(h, k)], r1.at[h, j - 1, k], on_first[h](j))
    banded, total = {}, [None, None]
    for k in (1, 2, 3, 0):
        for h in range(2):
            total[h] = gsend[group_at(h, 0), band_at(h, k)].astype(F32)
            for j in range(1, 4):
                scattered[h, j, k].wait_recv()
                total[h] = total[h] + r1[h, j - 1, k].astype(F32)
            if k > 0:
                s1[h, k - 1] = total[h].astype(BF)
                banded[h, k] = send(s1.at[h, k - 1], r2.at[h, k - 1], on_other[h](k))
    for h in range(2):
        for k in range(1, 4):
            banded[h, k].wait_recv()
            total[h] = total[h] + r2[h, k - 1].astype(F32)
        zbuf[z, h] = total[h].astype(BF)
    pl.semaphore_wait(ready, 1)
    crossed = [
        send(zbuf.at[z], zbuf.at[z], to(seg, time_of(lax.rem(z + k, 4), y, core), x)) for k in (2, 1, 3)
    ]
    for copy in crossed:
        copy.wait_recv()
    for h in range(2):
        summed = zbuf[0, h].astype(F32)
        for k in range(1, 4):
            summed = summed + zbuf[k, h].astype(F32)
        grad_ref[core, group_at(h, 0), band_at(h, 0)] = summed.astype(BF)

    over_other, over_first, over_pair = {}, {}, []
    for k in range(1, 4):
        for h in range(2):
            over_other[h, k] = send(piece(h, 0, 0), piece(h, 0, 0), on_other[h](k))
    for k in range(4):
        for h in range(2):
            if k > 0:
                over_other[h, k].wait_recv()
            held = piece(h, 0, (4 - k) % 4)
            for j in range(1, 4):
                over_first[h, j, k] = send(held, held, on_first[h](j))
            over_pair.append(send(held, held, partner))
    for k in range(4):
        for j in range(1, 4):
            for h in range(2):
                over_first[h, j, k].wait_recv()
                held = piece(h, 4 - j, (4 - k) % 4)
                over_pair.append(send(held, held, partner))
    for copy in over_pair:
        copy.wait_recv()

    for copy in started:
        copy.wait_send()
    v_swap.wait_send()

    @pl.when(core == 0)
    def _():
        u_to_one.wait_send()

    @pl.when(core == 1)
    def _():
        u_to_zero.wait_send()

    @pl.when(has_before)
    def _():
        slope_back.wait_send()

    @pl.when(plain_x)
    def _():
        own_x.wait_send()

    @pl.when(plain_d)
    def _():
        own_d.wait_send()

    @pl.when(bridge_after)
    def _():
        seam_x.wait_send()

    @pl.when(bridge_before)
    def _():
        seam_d.wait_send()

    for condition, copies in (
        (above, [straight for straight, _ in x_up]),
        (jnp.logical_and(above, has_after), [across for _, across in x_up]),
        (below, [straight for straight, _ in d_down]),
        (jnp.logical_and(below, has_before), [across for _, across in d_down]),
    ):

        @pl.when(condition)
        def _(copies=copies):
            for copy in copies:
                copy.wait_send()


def solution(mesh):
    S, T = mesh.shape["segment"], mesh.shape["tm"]
    Y = 4
    Z = T // (2 * Y)
    vmem, hbm = pl.BlockSpec(memory_space=pltpu.VMEM), pl.BlockSpec(memory_space=pltpu.HBM)
    cells = (FRAMES_HERE, 3, 16, 128)

    def body(features, score_cot, clip_frames, conv_weights, norm_gains, score_head):
        out, grad, back = pl.pallas_call(
            functools.partial(kernel, S, T, Y, Z),
            out_shape=(
                jax.ShapeDtypeStruct(cells, BF),
                jax.ShapeDtypeStruct((2, 28, 128, 128), BF),
                jax.ShapeDtypeStruct(cells, BF),
            ),
            in_specs=[
                hbm, hbm, hbm, hbm, hbm, hbm,
            ],
            out_specs=(vmem, vmem, vmem),
            scratch_shapes=[
                pltpu.VMEM((2, FRAMES_HERE, 3, 8, 128), BF),
                pltpu.VMEM((2, 3, FRAMES_HERE, 8), F32),
                pltpu.SMEM((2,), jnp.int32),
                pltpu.VMEM((1, 128), F32),
                pltpu.VMEM((1, 128), F32),
                pltpu.VMEM(cells, BF),
                pltpu.VMEM((2, 3456, 128), BF),
                pltpu.VMEM((2, 3456, 128), BF),
                pltpu.VMEM((8, 3, 16, 128), BF),
                pltpu.VMEM((8, 3, 16, 128), BF),
                pltpu.VMEM((6, 3, 16, 128), F32),
                pltpu.VMEM((8, 5, 16, 384), BF),
                pltpu.VMEM((6, 5, 16, 384), BF),
                pltpu.VMEM((4, 3, 16, 128), BF),
                pltpu.VMEM((10, 3, 16, 128), BF),
                pltpu.VMEM((384, 512), BF),
                pltpu.VMEM((12, 5, 16, 128), BF),
                pltpu.VMEM((2, 3, 16, 128), BF),
                pltpu.VMEM((28, 128, 128), BF),
                pltpu.VMEM((2, 3, 4, GROUP, BAND, 128), BF),
                pltpu.VMEM((2, 3, GROUP, BAND, 128), BF),
                pltpu.VMEM((2, 3, GROUP, BAND, 128), BF),
                pltpu.VMEM((4, 2, GROUP, BAND, 128), BF),
                pltpu.SemaphoreType.DMA((6,)),
                pltpu.SemaphoreType.DMA((SENDS,)),
                pltpu.SemaphoreType.DMA((SENDS,)),
                pltpu.SemaphoreType.REGULAR,
            ],
            compiler_params=pltpu.CompilerParams(
                collective_id=0, has_side_effects=True, vmem_limit_bytes=56 * 1024 * 1024
            ),
            cost_estimate=pl.CostEstimate(flops=10**9, bytes_accessed=6 * 10**6, transcendentals=10**5),
        )(features, jnp.transpose(score_cot, (0, 2, 1, 3)), clip_frames, conv_weights, norm_gains, score_head.reshape(1, 128))

        def split_clips(cells):
            return jnp.transpose(cells.reshape(FRAMES_HERE, 3, 2, 8, 128), (2, 0, 1, 3, 4))[None]

        return split_clips(out), grad[:, :27].reshape(1, 2, 3456, 128), split_clips(back)

    return jax.shard_map(
        body,
        mesh=mesh,
        in_specs=(
            P("dp", "tm", None, None, None),
            P("dp", "tm", None, None),
            P("dp"),
            P("segment", None, None, None),
            P("segment", None),
            P(),
        ),
        out_specs=(
            P("segment", "dp", "tm", None, None, None),
            P("segment", None, None, None),
            P("segment", "dp", "tm", None, None, None),
        ),
        check_vma=False,
    )
```

```python
import functools

import jax
import jax.numpy as jnp
from jax import lax
from jax.experimental import pallas as pl
from jax.experimental.pallas import tpu as pltpu
from jax.sharding import PartitionSpec as P

norm_eps = 1e-06
FRAMES_HERE = 4
GROUP = 7
BAND = 16
SENDS = 112
BF, F32 = jnp.bfloat16, jnp.float32


def column_shifts(values):
    shape = values.shape
    flat = values.reshape(-1, 8, 128)
    column = lax.broadcasted_iota(jnp.int32, flat.shape, 1)
    before = jnp.where(column == 0, 0.0, pltpu.roll(flat, 1, 1))
    after = jnp.where(column == 7, 0.0, pltpu.roll(flat, 7, 1))
    return [before.reshape(shape), values, after.reshape(shape)]


def fill(patch_ref, values):
    frames = values.shape[0]
    for e, shifted in enumerate(column_shifts(values)):
        patch_ref[:frames, 1:4, :, e * 128 : (e + 1) * 128] = shifted.astype(BF)


def convolve(patch_ref, weight_ref, which, frames, at=0):
    total = None
    for a in range(3):
        for b in range(3):
            rows = patch_ref[at + a : at + a + frames, b : b + 3].reshape(frames * 48, 384)
            taps = weight_ref[which, (9 * a + 3 * b) * 128 : (9 * a + 3 * b + 3) * 128, :]
            part = jnp.dot(rows, taps, preferred_element_type=F32)
            total = part if total is None else total + part
    return total.reshape(frames, 3, 16, 128)


def kernel(
    S, T, Y, Z,
    feat_hbm, score_hbm, clip_hbm, weight_hbm, gain_hbm, head_hbm,
    out_ref, grad_ref, back_ref,
    feat_ref, score_ref, clip_ref, gain_ref, head_ref, own, weight, flipped, xin, din, slope, patch8, patch6, vsend, vbuf, vt, upad, pcot, gsend, r1, s1, r2, zbuf,
    local_sem, send_sem, recv_sem, ready,
):
    seg, t, x = lax.axis_index("segment"), lax.axis_index("tm"), lax.axis_index("dp")
    core = lax.rem(t, 2)
    y = lax.rem(t // 2, Y)
    z = t // (2 * Y)
    frames = FRAMES_HERE

    def time_of(z, y, core):
        return (z * Y + y) * 2 + core

    def to(seg_to, t_to, x_to):
        return {"segment": seg_to, "tm": t_to, "dp": x_to}

    def remote(source, target, send, recv, device):
        return pltpu.make_async_remote_copy(
            src_ref=source, dst_ref=target, send_sem=send_sem.at[send], recv_sem=recv_sem.at[recv],
            device_id=device, device_id_type=pl.DeviceIdType.MESH,
        )

    loads = [
        pltpu.make_async_copy(source, target, local_sem.at[i])
        for i, (source, target) in enumerate((
            (feat_hbm, feat_ref), (gain_hbm, gain_ref), (weight_hbm.at[0], weight),
            (score_hbm, score_ref), (clip_hbm, clip_ref), (head_hbm, head_ref),
        ))
    ]
    for load in loads:
        load.start()

    patch8[:, 0] = jnp.zeros_like(patch8[:, 0])
    patch8[:, 4] = jnp.zeros_like(patch8[:, 4])
    patch6[:, 0] = jnp.zeros_like(patch6[:, 0])
    patch6[:, 4] = jnp.zeros_like(patch6[:, 4])
    upad[...] = jnp.zeros_like(upad)
    gsend[27] = jnp.zeros_like(gsend[27])
    has_before, has_after = t > 0, t < T - 1
    seam_after = jnp.logical_and(has_after, lax.rem(t, 2 * Y) == 2 * Y - 1)
    seam_before = jnp.logical_and(has_before, lax.rem(t, 2 * Y) == 0)
    bridge_after = jnp.logical_and(seg == S - 1, seam_after)
    bridge_before = jnp.logical_and(seg == 0, seam_before)
    below, above = seg > 0, seg < S - 1
    before, after = jnp.maximum(t - 1, 0), jnp.minimum(t + 1, T - 1)
    lower, upper = jnp.maximum(seg - 1, 0), jnp.minimum(seg + 1, S - 1)

    @pl.when(jnp.logical_not(has_before))
    def _():
        xin[0:frames] = jnp.zeros_like(xin[0:frames])

    @pl.when(jnp.logical_not(has_after))
    def _():
        din[frames:] = jnp.zeros_like(din[frames:])
        slope[frames:] = jnp.zeros_like(slope[frames:])

    barrier = pltpu.get_barrier_semaphore()
    expected = 8
    for condition, device in (
        (has_before, to(seg, before, x)),
        (has_after, to(seg, after, x)),
        (above, to(upper, t, x)),
        (jnp.logical_and(above, has_after), to(upper, after, x)),
        (below, to(lower, t, x)),
        (jnp.logical_and(below, has_before), to(lower, before, x)),
        (bridge_after, to(0, after, x)),
        (bridge_before, to(S - 1, before, x)),
    ):
        expected = expected + condition.astype(jnp.int32)

        @pl.when(condition)
        def _(device=device):
            pl.semaphore_signal(barrier, 1, device_id=device, device_id_type=pl.DeviceIdType.MESH)

    for device in [
        *(to(seg, t, lax.rem(x + step, 4)) for step in range(1, 4)),
        *(to(seg, time_of(z, lax.rem(y + step, 4), core), x) for step in range(1, 4)),
        *(to(seg, time_of(lax.rem(z + step, 4), y, core), x) for step in (1, 3)),
    ]:
        pl.semaphore_signal(barrier, 1, device_id=device, device_id_type=pl.DeviceIdType.MESH)

    def put_features(target):
        target[...] = jnp.concatenate([feat_ref[0].astype(F32), feat_ref[1].astype(F32)], axis=2).astype(BF)

    def put_seeds(target):
        eye = lax.broadcasted_iota(jnp.int32, (8, 8), 0) == lax.broadcasted_iota(jnp.int32, (8, 8), 1)
        head = head_ref[...]
        for f in range(frames):
            for i in range(3):
                halves = []
                for n in range(2):
                    line = score_ref[n, i, f : f + 1, :]
                    valid = jnp.where(t * frames + f < clip_ref[n], 1.0, 0.0)
                    stood = jnp.sum(jnp.where(eye, jnp.broadcast_to(line, (8, 8)), 0.0), axis=1, keepdims=True)
                    halves.append((stood * valid) * head)
                target[f, i] = jnp.concatenate(halves, axis=0).astype(BF)

    for load in loads:
        load.wait()

    @pl.when(seg == 0)
    def _():
        put_features(xin.at[pl.ds(frames, frames)])

    @pl.when(seg == S - 1)
    def _():
        put_features(own)
        put_seeds(din.at[pl.ds(0, frames)])

    pl.semaphore_wait(barrier, expected)
    pl.semaphore_signal(
        ready, 1, device_id=to(seg, time_of(lax.rem(z + 3, 4), y, core), x), device_id_type=pl.DeviceIdType.MESH
    )

    own_x = remote(xin.at[pl.ds(frames, frames)], xin.at[pl.ds(0, frames)], 0, 0, to(seg, after, x))
    own_d = remote(din.at[pl.ds(0, frames)], din.at[pl.ds(frames, frames)], 1, 1, to(seg, before, x))
    seam_x = remote(own, xin.at[pl.ds(0, frames)], 0, 0, to(0, after, x))
    seam_d = remote(own, din.at[pl.ds(frames, frames)], 1, 1, to(S - 1, before, x))
    x_up, d_down = [], []
    for h in range(2):
        here, later = pl.ds(2 * h, 2), pl.ds(frames + 2 * h, 2)
        x_up.append((
            remote(out_ref.at[here], xin.at[later], 2 + h, 2 + h, to(upper, t, x)),
            remote(out_ref.at[here], xin.at[here], 4 + h, 4 + h, to(upper, after, x)),
        ))
        d_down.append((
            remote(back_ref.at[here], din.at[here], 6 + h, 6 + h, to(lower, t, x)),
            remote(back_ref.at[here], din.at[later], 8 + h, 8 + h, to(lower, before, x)),
        ))
    slope_back = remote(slope.at[pl.ds(0, 2)], slope.at[pl.ds(4, 2)], 10, 10, to(seg, before, x))
    partner = to(seg, t + 1 - 2 * core, x)
    v_swap = remote(vsend, vbuf.at[pl.ds(6 * core, 4)], 11, 11, partner)
    u_to_one = remote(din.at[pl.ds(0, 4)], upad.at[pl.ds(2, 4), pl.ds(1, 3)], 12, 12, partner)
    u_to_zero = remote(pcot, upad.at[pl.ds(8, 2), pl.ds(1, 3)], 12, 12, partner)
    plain_x = jnp.logical_and(seg == 0, jnp.logical_and(has_after, jnp.logical_not(seam_after)))
    plain_d = jnp.logical_and(seg == S - 1, jnp.logical_and(has_before, jnp.logical_not(seam_before)))

    @pl.when(plain_x)
    def _():
        own_x.start()

    @pl.when(bridge_after)
    def _():
        seam_x.start()

    @pl.when(plain_d)
    def _():
        own_d.start()

    def flip_all():
        def one(i, carry):
            source = pl.multiple_of(i * 128, 128)
            target = pl.multiple_of((26 - i) * 128, 128)
            for which in range(2):
                tap = weight[which, pl.ds(source, 128), :].astype(F32)
                flipped[which, pl.ds(target, 128), :] = tap.T.astype(BF)
            return carry

        lax.fori_loop(0, 27, one, 0)

    @pl.when(below)
    def _():
        flip_all()

    @pl.when(below)
    def _():
        for straight, _ in x_up:
            straight.wait_recv()

    @pl.when(jnp.logical_and(below, has_before))
    def _():
        for _, across in x_up:
            across.wait_recv()

    @pl.when(jnp.logical_and(seg == 0, has_before))
    def _():
        own_x.wait_recv()

    gain = gain_ref[...]
    wide = xin[...].astype(F32)
    root = lax.rsqrt(jnp.mean(wide * wide, axis=-1, keepdims=True) + norm_eps)
    normed = (wide * root * gain).astype(BF).astype(F32)
    fill(patch8, normed)
    pre = convolve(patch8, weight, 0, 6)
    sig = 1.0 / (1.0 + jnp.exp(-pre))
    hidden = (pre * sig).astype(BF).astype(F32)
    slope[0:4] = (sig * (1.0 + pre * (1.0 - sig)))[2:6]

    @pl.when(has_before)
    def _():
        slope_back.start()

    fill(patch6, hidden)
    vsend[...] = jnp.where(core == 0, hidden[0:4], normed[4:8]).astype(BF)
    vbuf[pl.ds(4 * core, 6)] = jnp.where(core == 0, normed[2:8], hidden).astype(BF)
    v_swap.start()
    for h in range(2):
        rows = slice(2 * h, 2 * h + 2)
        second = convolve(patch6, weight, 1, 2, 2 * h)
        out_ref[rows] = (xin[4 + 2 * h : 6 + 2 * h].astype(F32) + second).astype(BF)

        @pl.when(jnp.logical_and(above, has_after))
        def _(h=h):
            x_up[h][1].start()

        @pl.when(above)
        def _(h=h):
            x_up[h][0].start()

    def stand_up():
        v_swap.wait_recv()
        flat = vbuf[...].astype(F32)
        for e, shifted in enumerate(column_shifts(flat)):
            rows = jnp.concatenate([shifted.reshape(480, 128), jnp.zeros((32, 128), F32)], axis=0)
            vt[e * 128 : (e + 1) * 128, :] = rows.T.astype(BF)

    @pl.when(bridge_before)
    def _():
        put_seeds(own)
        seam_d.start()

    @pl.when(seg == 0)
    def _():
        flip_all()

    @pl.when(above)
    def _():
        stand_up()

    @pl.when(above)
    def _():
        for straight, _ in d_down:
            straight.wait_recv()

    @pl.when(core == 0)
    def _():
        u_to_one.start()

    @pl.when(core == 1)
    def _():
        upad[6:10, 1:4] = din[0:4]

    @pl.when(jnp.logical_and(above, has_after))
    def _():
        for _, across in d_down:
            across.wait_recv()

    @pl.when(jnp.logical_and(seg == S - 1, has_after))
    def _():
        own_d.wait_recv()

    fill(patch8, din[...].astype(F32))
    hidden_cot = convolve(patch8, flipped, 1, 6)

    @pl.when(has_after)
    def _():
        slope_back.wait_recv()

    pre_cot = (hidden_cot * slope[...]).astype(BF)

    @pl.when(core == 0)
    def _():
        upad[2:8, 1:4] = pre_cot

    @pl.when(core == 1)
    def _():
        pcot[...] = pre_cot[2:4]
        u_to_zero.start()

    fill(patch6, pre_cot.astype(F32))
    for h in range(2):
        rows = slice(2 * h, 2 * h + 2)
        normed_cot = convolve(patch6, flipped, 0, 2, 2 * h)
        wide = xin[4 + 2 * h : 6 + 2 * h].astype(F32)
        root = lax.rsqrt(jnp.mean(wide * wide, axis=-1, keepdims=True) + norm_eps)
        weighted = normed_cot * gain
        inner = jnp.mean(weighted * wide, axis=-1, keepdims=True)
        back_ref[rows] = (din[rows].astype(F32) + (root * weighted - wide * root * root * root * inner)).astype(BF)

        @pl.when(jnp.logical_and(below, has_before))
        def _(h=h):
            d_down[h][1].start()

        @pl.when(below)
        def _(h=h):
            d_down[h][0].start()

    @pl.when(seg == S - 1)
    def _():
        stand_up()

    def on_x(step):
        return to(seg, t, lax.rem(x + step, 4))

    def on_y(step):
        return to(seg, time_of(z, lax.rem(y + step, 4), core), x)

    first, other = (x, y), (y, x)
    on_first, on_other = (on_x, on_y), (on_y, on_x)

    def group_at(h, step):
        return pl.ds(lax.rem(first[h] + step, 4) * GROUP, GROUP)

    def band_at(h, step):
        return pl.ds(pl.multiple_of(64 * h + lax.rem(other[h] + step, 4) * BAND, BAND), BAND)

    def piece(h, j, k):
        return grad_ref.at[core, group_at(h, j), band_at(h, k)]

    @pl.when(core == 0)
    def _():
        u_to_zero.wait_recv()

    @pl.when(core == 1)
    def _():
        u_to_one.wait_recv()

    for a in range(3):
        for b in range(3):
            rows = upad[2 - a : 12 - a, 2 - b : 5 - b].reshape(480, 128)
            rows = jnp.concatenate([rows, jnp.zeros((32, 128), BF)], axis=0)
            part = jnp.dot(vt[...], rows, preferred_element_type=F32)
            gsend[9 * a + 3 * b : 9 * a + 3 * b + 3] = part.astype(BF).reshape(3, 128, 128)

    started = []

    def send(source, target, device):
        index = len(started)
        copy = remote(source, target, 13 + index, 13 + index, device)
        copy.start()
        started.append(copy)
        return copy

    scattered = {}
    for k in (1, 2, 3, 0):
        for j in range(1, 4):
            for h in range(2):
                scattered[h, j, k] = send(gsend.at[group_at(h, j), band_at(h, k)], r1.at[h, j - 1, k], on_first[h](j))
    banded, total = {}, [None, None]
    for k in (1, 2, 3, 0):
        for h in range(2):
            total[h] = gsend[group_at(h, 0), band_at(h, k)].astype(F32)
            for j in range(1, 4):
                scattered[h, j, k].wait_recv()
                total[h] = total[h] + r1[h, j - 1, k].astype(F32)
            if k > 0:
                s1[h, k - 1] = total[h].astype(BF)
                banded[h, k] = send(s1.at[h, k - 1], r2.at[h, k - 1], on_other[h](k))
    for h in range(2):
        for k in range(1, 4):
            banded[h, k].wait_recv()
            total[h] = total[h] + r2[h, k - 1].astype(F32)
        zbuf[z, h] = total[h].astype(BF)
    pl.semaphore_wait(ready, 1)
    crossed = [
        send(zbuf.at[z], zbuf.at[z], to(seg, time_of(lax.rem(z + k, 4), y, core), x)) for k in (2, 1, 3)
    ]
    for copy in crossed:
        copy.wait_recv()
    for h in range(2):
        summed = zbuf[0, h].astype(F32)
        for k in range(1, 4):
            summed = summed + zbuf[k, h].astype(F32)
        grad_ref[core, group_at(h, 0), band_at(h, 0)] = summed.astype(BF)

    over_other, over_first, over_pair = {}, {}, []
    for k in range(1, 4):
        for h in range(2):
            over_other[h, k] = send(piece(h, 0, 0), piece(h, 0, 0), on_other[h](k))
    for k in range(4):
        for h in range(2):
            if k > 0:
                over_other[h, k].wait_recv()
            held = piece(h, 0, (4 - k) % 4)
            for j in range(1, 4):
                over_first[h, j, k] = send(held, held, on_first[h](j))
            over_pair.append(send(held, held, partner))
    for k in range(4):
        for j in range(1, 4):
            for h in range(2):
                over_first[h, j, k].wait_recv()
                held = piece(h, 4 - j, (4 - k) % 4)
                over_pair.append(send(held, held, partner))
    for copy in over_pair:
        copy.wait_recv()

    for copy in started:
        copy.wait_send()
    v_swap.wait_send()

    @pl.when(core == 0)
    def _():
        u_to_one.wait_send()

    @pl.when(core == 1)
    def _():
        u_to_zero.wait_send()

    @pl.when(has_before)
    def _():
        slope_back.wait_send()

    @pl.when(plain_x)
    def _():
        own_x.wait_send()

    @pl.when(plain_d)
    def _():
        own_d.wait_send()

    @pl.when(bridge_after)
    def _():
        seam_x.wait_send()

    @pl.when(bridge_before)
    def _():
        seam_d.wait_send()

    for condition, copies in (
        (above, [straight for straight, _ in x_up]),
        (jnp.logical_and(above, has_after), [across for _, across in x_up]),
        (below, [straight for straight, _ in d_down]),
        (jnp.logical_and(below, has_before), [across for _, across in d_down]),
    ):

        @pl.when(condition)
        def _(copies=copies):
            for copy in copies:
                copy.wait_send()


def solution(mesh):
    S, T = mesh.shape["segment"], mesh.shape["tm"]
    Y = 4
    Z = T // (2 * Y)
    vmem, hbm = pl.BlockSpec(memory_space=pltpu.VMEM), pl.BlockSpec(memory_space=pltpu.HBM)
    cells = (FRAMES_HERE, 3, 16, 128)

    def body(features, score_cot, clip_frames, conv_weights, norm_gains, score_head):
        out, grad, back = pl.pallas_call(
            functools.partial(kernel, S, T, Y, Z),
            out_shape=(
                jax.ShapeDtypeStruct(cells, BF),
                jax.ShapeDtypeStruct((2, 28, 128, 128), BF),
                jax.ShapeDtypeStruct(cells, BF),
            ),
            in_specs=[
                hbm, hbm, hbm, hbm, hbm, hbm,
            ],
            out_specs=(vmem, vmem, vmem),
            scratch_shapes=[
                pltpu.VMEM((2, FRAMES_HERE, 3, 8, 128), BF),
                pltpu.VMEM((2, 3, FRAMES_HERE, 8), F32),
                pltpu.SMEM((2,), jnp.int32),
                pltpu.VMEM((1, 128), F32),
                pltpu.VMEM((1, 128), F32),
                pltpu.VMEM(cells, BF),
                pltpu.VMEM((2, 3456, 128), BF),
                pltpu.VMEM((2, 3456, 128), BF),
                pltpu.VMEM((8, 3, 16, 128), BF),
                pltpu.VMEM((8, 3, 16, 128), BF),
                pltpu.VMEM((6, 3, 16, 128), F32),
                pltpu.VMEM((8, 5, 16, 384), BF),
                pltpu.VMEM((6, 5, 16, 384), BF),
                pltpu.VMEM((4, 3, 16, 128), BF),
                pltpu.VMEM((10, 3, 16, 128), BF),
                pltpu.VMEM((384, 512), BF),
                pltpu.VMEM((12, 5, 16, 128), BF),
                pltpu.VMEM((2, 3, 16, 128), BF),
                pltpu.VMEM((28, 128, 128), BF),
                pltpu.VMEM((2, 3, 4, GROUP, BAND, 128), BF),
                pltpu.VMEM((2, 3, GROUP, BAND, 128), BF),
                pltpu.VMEM((2, 3, GROUP, BAND, 128), BF),
                pltpu.VMEM((4, 2, GROUP, BAND, 128), BF),
                pltpu.SemaphoreType.DMA((6,)),
                pltpu.SemaphoreType.DMA((SENDS,)),
                pltpu.SemaphoreType.DMA((SENDS,)),
                pltpu.SemaphoreType.REGULAR,
            ],
            compiler_params=pltpu.CompilerParams(
                collective_id=0, has_side_effects=True, vmem_limit_bytes=40 * 1024 * 1024
            ),
            cost_estimate=pl.CostEstimate(flops=10**9, bytes_accessed=6 * 10**6, transcendentals=10**5),
        )(*(
            pltpu.with_memory_space_constraint(array, pltpu.HBM)
            for array in (
                features, jnp.transpose(score_cot, (0, 2, 1, 3)), clip_frames, conv_weights, norm_gains,
                score_head.reshape(1, 128),
            )
        ))

        def split_clips(cells):
            return jnp.transpose(cells.reshape(FRAMES_HERE, 3, 2, 8, 128), (2, 0, 1, 3, 4))[None]

        return split_clips(out), grad[:, :27].reshape(1, 2, 3456, 128), split_clips(back)

    return jax.shard_map(
        body,
        mesh=mesh,
        in_specs=(
            P("dp", "tm", None, None, None),
            P("dp", "tm", None, None),
            P("dp"),
            P("segment", None, None, None),
            P("segment", None),
            P(),
        ),
        out_specs=(
            P("segment", "dp", "tm", None, None, None),
            P("segment", None, None, None),
            P("segment", "dp", "tm", None, None, None),
        ),
        check_vma=False,
    )
```

```python
import functools

import jax
import jax.numpy as jnp
from jax import lax
from jax.experimental import pallas as pl
from jax.experimental.pallas import tpu as pltpu
from jax.sharding import PartitionSpec as P

norm_eps = 1e-06
FRAMES_HERE = 4
GROUP = 7
BAND = 16
SENDS = 112
BF, F32 = jnp.bfloat16, jnp.float32


def column_shifts(values):
    shape = values.shape
    flat = values.reshape(-1, 8, 128)
    column = lax.broadcasted_iota(jnp.int32, flat.shape, 1)
    before = jnp.where(column == 0, 0.0, pltpu.roll(flat, 1, 1))
    after = jnp.where(column == 7, 0.0, pltpu.roll(flat, 7, 1))
    return [before.reshape(shape), values, after.reshape(shape)]


def fill(patch_ref, values, at=0):
    frames = values.shape[0]
    for e, shifted in enumerate(column_shifts(values)):
        patch_ref[at : at + frames, 1:4, :, e * 128 : (e + 1) * 128] = shifted.astype(BF)


def convolve(patch_ref, weight_ref, which, frames, at=0):
    total = None
    for a in range(3):
        for b in range(3):
            rows = patch_ref[at + a : at + a + frames, b : b + 3].reshape(frames * 48, 384)
            taps = weight_ref[which, (9 * a + 3 * b) * 128 : (9 * a + 3 * b + 3) * 128, :]
            part = jnp.dot(rows, taps, preferred_element_type=F32)
            total = part if total is None else total + part
    return total.reshape(frames, 3, 16, 128)


def kernel(
    S, T, Y, Z,
    feat_hbm, score_hbm, clip_hbm, weight_hbm, gain_hbm, head_hbm,
    out_ref, grad_ref, back_ref,
    feat_ref, score_ref, clip_ref, gain_ref, head_ref, own, weight, flipped, xin, din, slope, patch8, patch6, patchb, hcot, vsend, vbuf, vt, upad, pcot, gsend, r1, s1, r2, zbuf,
    local_sem, send_sem, recv_sem, ready,
):
    seg, t, x = lax.axis_index("segment"), lax.axis_index("tm"), lax.axis_index("dp")
    core = lax.rem(t, 2)
    y = lax.rem(t // 2, Y)
    z = t // (2 * Y)
    frames = FRAMES_HERE

    def time_of(z, y, core):
        return (z * Y + y) * 2 + core

    def to(seg_to, t_to, x_to):
        return {"segment": seg_to, "tm": t_to, "dp": x_to}

    def remote(source, target, send, recv, device):
        return pltpu.make_async_remote_copy(
            src_ref=source, dst_ref=target, send_sem=send_sem.at[send], recv_sem=recv_sem.at[recv],
            device_id=device, device_id_type=pl.DeviceIdType.MESH,
        )

    loads = [
        pltpu.make_async_copy(source, target, local_sem.at[i])
        for i, (source, target) in enumerate((
            (feat_hbm, feat_ref), (gain_hbm, gain_ref), (weight_hbm.at[0], weight),
            (score_hbm, score_ref), (clip_hbm, clip_ref), (head_hbm, head_ref),
        ))
    ]
    for load in loads:
        load.start()

    patch8[:, 0] = jnp.zeros_like(patch8[:, 0])
    patch8[:, 4] = jnp.zeros_like(patch8[:, 4])
    patch6[:, 0] = jnp.zeros_like(patch6[:, 0])
    patch6[:, 4] = jnp.zeros_like(patch6[:, 4])
    patchb[:, 0] = jnp.zeros_like(patchb[:, 0])
    patchb[:, 4] = jnp.zeros_like(patchb[:, 4])
    upad[...] = jnp.zeros_like(upad)
    gsend[27] = jnp.zeros_like(gsend[27])
    has_before, has_after = t > 0, t < T - 1
    seam_after = jnp.logical_and(has_after, lax.rem(t, 2 * Y) == 2 * Y - 1)
    seam_before = jnp.logical_and(has_before, lax.rem(t, 2 * Y) == 0)
    bridge_after = jnp.logical_and(seg == S - 1, seam_after)
    bridge_before = jnp.logical_and(seg == 0, seam_before)
    ahead_to = jnp.logical_and(seg == S - 2, has_before)
    ahead_from = jnp.logical_and(seg == S - 1, has_after)
    below, above = seg > 0, seg < S - 1
    before, after = jnp.maximum(t - 1, 0), jnp.minimum(t + 1, T - 1)
    lower, upper = jnp.maximum(seg - 1, 0), jnp.minimum(seg + 1, S - 1)

    @pl.when(jnp.logical_not(has_before))
    def _():
        xin[0:frames] = jnp.zeros_like(xin[0:frames])

    @pl.when(jnp.logical_not(has_after))
    def _():
        din[frames:] = jnp.zeros_like(din[frames:])
        xin[8:10] = jnp.zeros_like(xin[8:10])
        slope[frames:] = jnp.zeros_like(slope[frames:])

    barrier = pltpu.get_barrier_semaphore()
    expected = 8
    for condition, device in (
        (has_before, to(seg, before, x)),
        (has_after, to(seg, after, x)),
        (above, to(upper, t, x)),
        (jnp.logical_and(above, has_after), to(upper, after, x)),
        (below, to(lower, t, x)),
        (jnp.logical_and(below, has_before), to(lower, before, x)),
        (bridge_after, to(0, after, x)),
        (bridge_before, to(S - 1, before, x)),
        (ahead_to, to(S - 1, before, x)),
        (ahead_from, to(S - 2, after, x)),
    ):
        expected = expected + condition.astype(jnp.int32)

        @pl.when(condition)
        def _(device=device):
            pl.semaphore_signal(barrier, 1, device_id=device, device_id_type=pl.DeviceIdType.MESH)

    for device in [
        *(to(seg, t, lax.rem(x + step, 4)) for step in range(1, 4)),
        *(to(seg, time_of(z, lax.rem(y + step, 4), core), x) for step in range(1, 4)),
        *(to(seg, time_of(lax.rem(z + step, 4), y, core), x) for step in (1, 3)),
    ]:
        pl.semaphore_signal(barrier, 1, device_id=device, device_id_type=pl.DeviceIdType.MESH)

    def put_features(target):
        target[...] = jnp.concatenate([feat_ref[0].astype(F32), feat_ref[1].astype(F32)], axis=2).astype(BF)

    def put_seeds(target):
        eye = lax.broadcasted_iota(jnp.int32, (8, 8), 0) == lax.broadcasted_iota(jnp.int32, (8, 8), 1)
        head = head_ref[...]
        for f in range(frames):
            for i in range(3):
                halves = []
                for n in range(2):
                    line = score_ref[n, i, f : f + 1, :]
                    valid = jnp.where(t * frames + f < clip_ref[n], 1.0, 0.0)
                    stood = jnp.sum(jnp.where(eye, jnp.broadcast_to(line, (8, 8)), 0.0), axis=1, keepdims=True)
                    halves.append((stood * valid) * head)
                target[f, i] = jnp.concatenate(halves, axis=0).astype(BF)

    for load in loads:
        load.wait()

    @pl.when(seg == 0)
    def _():
        put_features(xin.at[pl.ds(frames, frames)])

    @pl.when(seg == S - 1)
    def _():
        put_features(own)
        put_seeds(din.at[pl.ds(0, frames)])

    pl.semaphore_wait(barrier, expected)
    pl.semaphore_signal(
        ready, 1, device_id=to(seg, time_of(lax.rem(z + 3, 4), y, core), x), device_id_type=pl.DeviceIdType.MESH
    )

    x_ahead = remote(out_ref.at[pl.ds(0, 2)], xin.at[pl.ds(8, 2)], 110, 110, to(S - 1, before, x))
    own_x = remote(xin.at[pl.ds(frames, frames)], xin.at[pl.ds(0, frames)], 0, 0, to(seg, after, x))
    own_d = remote(din.at[pl.ds(0, frames)], din.at[pl.ds(frames, frames)], 1, 1, to(seg, before, x))
    seam_x = remote(own, xin.at[pl.ds(0, frames)], 0, 0, to(0, after, x))
    seam_d = remote(own, din.at[pl.ds(frames, frames)], 1, 1, to(S - 1, before, x))
    x_up, d_down = [], []
    for h in range(2):
        here, later = pl.ds(2 * h, 2), pl.ds(frames + 2 * h, 2)
        x_up.append((
            remote(out_ref.at[here], xin.at[later], 2 + h, 2 + h, to(upper, t, x)),
            remote(out_ref.at[here], xin.at[here], 4 + h, 4 + h, to(upper, after, x)),
        ))
        d_down.append((
            remote(back_ref.at[here], din.at[here], 6 + h, 6 + h, to(lower, t, x)),
            remote(back_ref.at[here], din.at[later], 8 + h, 8 + h, to(lower, before, x)),
        ))
    slope_back = remote(slope.at[pl.ds(0, 2)], slope.at[pl.ds(4, 2)], 10, 10, to(seg, before, x))
    partner = to(seg, t + 1 - 2 * core, x)
    v_swap = remote(vsend, vbuf.at[pl.ds(6 * core, 4)], 11, 11, partner)
    u_to_one = remote(din.at[pl.ds(0, 4)], upad.at[pl.ds(2, 4), pl.ds(1, 3)], 12, 12, partner)
    u_to_zero = remote(pcot, upad.at[pl.ds(8, 2), pl.ds(1, 3)], 12, 12, partner)
    plain_x = jnp.logical_and(seg == 0, jnp.logical_and(has_after, jnp.logical_not(seam_after)))
    plain_d = jnp.logical_and(seg == S - 1, jnp.logical_and(has_before, jnp.logical_not(seam_before)))

    @pl.when(plain_x)
    def _():
        own_x.start()

    @pl.when(bridge_after)
    def _():
        seam_x.start()

    @pl.when(plain_d)
    def _():
        own_d.start()

    def flip_all():
        def one(i, carry):
            source = pl.multiple_of(i * 128, 128)
            target = pl.multiple_of((26 - i) * 128, 128)
            for which in range(2):
                tap = weight[which, pl.ds(source, 128), :].astype(F32)
                flipped[which, pl.ds(target, 128), :] = tap.T.astype(BF)
            return carry

        lax.fori_loop(0, 27, one, 0)

    @pl.when(below)
    def _():
        flip_all()

    def hidden_back():
        fill(patch8, din[...].astype(F32))
        hcot[...] = convolve(patch8, flipped, 1, 6)

    @pl.when(jnp.logical_and(seg == S - 1, has_after))
    def _():
        own_d.wait_recv()

    @pl.when(seg == S - 1)
    def _():
        hidden_back()

    @pl.when(below)
    def _():
        for straight, _ in x_up:
            straight.wait_recv()

    @pl.when(jnp.logical_and(below, has_before))
    def _():
        for _, across in x_up:
            across.wait_recv()

    @pl.when(jnp.logical_and(seg == 0, has_before))
    def _():
        own_x.wait_recv()

    gain = gain_ref[...]

    def normalize(values):
        wide = values.astype(F32)
        root = lax.rsqrt(jnp.mean(wide * wide, axis=-1, keepdims=True) + norm_eps)
        return (wide * root * gain).astype(BF).astype(F32)

    normed = normalize(xin[0:8])
    fill(patch8, normed)
    pre = convolve(patch8, weight, 0, 6)
    sig = 1.0 / (1.0 + jnp.exp(-pre))
    hidden = (pre * sig).astype(BF).astype(F32)
    slope[0:4] = (sig * (1.0 + pre * (1.0 - sig)))[2:6]

    @pl.when(ahead_from)
    def _():
        x_ahead.wait_recv()

    @pl.when(seg == S - 1)
    def _():
        fill(patch8, normalize(xin[8:10]), 8)
        later = convolve(patch8, weight, 0, 2, 6)
        share = 1.0 / (1.0 + jnp.exp(-later))
        slope[4:6] = share * (1.0 + later * (1.0 - share))

    slope_to, slope_from = jnp.logical_and(above, has_before), jnp.logical_and(above, has_after)

    @pl.when(slope_to)
    def _():
        slope_back.start()

    fill(patch6, hidden)
    vsend[...] = jnp.where(core == 0, hidden[0:4], normed[4:8]).astype(BF)
    vbuf[pl.ds(4 * core, 6)] = jnp.where(core == 0, normed[2:8], hidden).astype(BF)
    v_swap.start()
    def second_half():
        for h in range(2):
            rows = slice(2 * h, 2 * h + 2)
            second = convolve(patch6, weight, 1, 2, 2 * h)
            out_ref[rows] = (xin[4 + 2 * h : 6 + 2 * h].astype(F32) + second).astype(BF)

            @pl.when(jnp.logical_and(above, has_after))
            def _(h=h):
                x_up[h][1].start()

            @pl.when(above)
            def _(h=h):
                x_up[h][0].start()

            if h == 0:

                @pl.when(ahead_to)
                def _():
                    x_ahead.start()

    @pl.when(above)
    def _():
        second_half()

    def stand_up():
        v_swap.wait_recv()
        flat = vbuf[...].astype(F32)
        for e, shifted in enumerate(column_shifts(flat)):
            rows = jnp.concatenate([shifted.reshape(480, 128), jnp.zeros((32, 128), F32)], axis=0)
            vt[e * 128 : (e + 1) * 128, :] = rows.T.astype(BF)

    @pl.when(bridge_before)
    def _():
        put_seeds(own)
        seam_d.start()

    @pl.when(seg == 0)
    def _():
        flip_all()

    @pl.when(above)
    def _():
        stand_up()

    @pl.when(above)
    def _():
        for straight, _ in d_down:
            straight.wait_recv()

    @pl.when(core == 0)
    def _():
        u_to_one.start()

    @pl.when(core == 1)
    def _():
        upad[6:10, 1:4] = din[0:4]

    @pl.when(jnp.logical_and(above, has_after))
    def _():
        for _, across in d_down:
            across.wait_recv()

    @pl.when(above)
    def _():
        hidden_back()

    @pl.when(slope_from)
    def _():
        slope_back.wait_recv()

    pre_cot = (hcot[...] * slope[...]).astype(BF)

    @pl.when(core == 0)
    def _():
        upad[2:8, 1:4] = pre_cot

    @pl.when(core == 1)
    def _():
        pcot[...] = pre_cot[2:4]
        u_to_zero.start()

    fill(patchb, pre_cot.astype(F32))

    def input_back():
        for h in range(2):
            rows = slice(2 * h, 2 * h + 2)
            normed_cot = convolve(patchb, flipped, 0, 2, 2 * h)
            wide = xin[4 + 2 * h : 6 + 2 * h].astype(F32)
            root = lax.rsqrt(jnp.mean(wide * wide, axis=-1, keepdims=True) + norm_eps)
            weighted = normed_cot * gain
            inner = jnp.mean(weighted * wide, axis=-1, keepdims=True)
            back_ref[rows] = (din[rows].astype(F32) + (root * weighted - wide * root * root * root * inner)).astype(BF)

            @pl.when(jnp.logical_and(below, has_before))
            def _(h=h):
                d_down[h][1].start()

            @pl.when(below)
            def _(h=h):
                d_down[h][0].start()

    postponed = jnp.logical_and(seg == 0, core == 1)

    @pl.when(jnp.logical_not(postponed))
    def _():
        input_back()

    @pl.when(seg == S - 1)
    def _():
        second_half()
        stand_up()

    def on_x(step):
        return to(seg, t, lax.rem(x + step, 4))

    def on_y(step):
        return to(seg, time_of(z, lax.rem(y + step, 4), core), x)

    first, other = (x, y), (y, x)
    on_first, on_other = (on_x, on_y), (on_y, on_x)

    def group_at(h, step):
        return pl.ds(lax.rem(first[h] + step, 4) * GROUP, GROUP)

    def band_at(h, step):
        return pl.ds(pl.multiple_of(64 * h + lax.rem(other[h] + step, 4) * BAND, BAND), BAND)

    def piece(h, j, k):
        return grad_ref.at[core, group_at(h, j), band_at(h, k)]

    @pl.when(core == 0)
    def _():
        u_to_zero.wait_recv()

    @pl.when(core == 1)
    def _():
        u_to_one.wait_recv()

    for a in range(3):
        for b in range(3):
            rows = upad[2 - a : 12 - a, 2 - b : 5 - b].reshape(480, 128)
            rows = jnp.concatenate([rows, jnp.zeros((32, 128), BF)], axis=0)
            part = jnp.dot(vt[...], rows, preferred_element_type=F32)
            gsend[9 * a + 3 * b : 9 * a + 3 * b + 3] = part.astype(BF).reshape(3, 128, 128)

    started = []

    def send(source, target, device):
        index = len(started)
        copy = remote(source, target, 13 + index, 13 + index, device)
        copy.start()
        started.append(copy)
        return copy

    scattered = {}
    for k in (1, 2, 3, 0):
        for j in range(1, 4):
            for h in range(2):
                scattered[h, j, k] = send(gsend.at[group_at(h, j), band_at(h, k)], r1.at[h, j - 1, k], on_first[h](j))

    @pl.when(postponed)
    def _():
        input_back()

    banded, total = {}, [None, None]
    for k in (1, 2, 3, 0):
        for h in range(2):
            total[h] = gsend[group_at(h, 0), band_at(h, k)].astype(F32)
            for j in range(1, 4):
                scattered[h, j, k].wait_recv()
                total[h] = total[h] + r1[h, j - 1, k].astype(F32)
            if k > 0:
                s1[h, k - 1] = total[h].astype(BF)
                banded[h, k] = send(s1.at[h, k - 1], r2.at[h, k - 1], on_other[h](k))
    for h in range(2):
        for k in range(1, 4):
            banded[h, k].wait_recv()
            total[h] = total[h] + r2[h, k - 1].astype(F32)
        zbuf[z, h] = total[h].astype(BF)
    pl.semaphore_wait(ready, 1)
    crossed = [
        send(zbuf.at[z], zbuf.at[z], to(seg, time_of(lax.rem(z + k, 4), y, core), x)) for k in (2, 1, 3)
    ]
    for copy in crossed:
        copy.wait_recv()
    for h in range(2):
        summed = zbuf[0, h].astype(F32)
        for k in range(1, 4):
            summed = summed + zbuf[k, h].astype(F32)
        grad_ref[core, group_at(h, 0), band_at(h, 0)] = summed.astype(BF)

    over_other, over_first, over_pair = {}, {}, []
    for k in range(1, 4):
        for h in range(2):
            over_other[h, k] = send(piece(h, 0, 0), piece(h, 0, 0), on_other[h](k))
    for k in range(4):
        for h in range(2):
            if k > 0:
                over_other[h, k].wait_recv()
            held = piece(h, 0, (4 - k) % 4)
            for j in range(1, 4):
                over_first[h, j, k] = send(held, held, on_first[h](j))
            over_pair.append(send(held, held, partner))
    for k in range(4):
        for j in range(1, 4):
            for h in range(2):
                over_first[h, j, k].wait_recv()
                held = piece(h, 4 - j, (4 - k) % 4)
                over_pair.append(send(held, held, partner))
    for copy in over_pair:
        copy.wait_recv()

    for copy in started:
        copy.wait_send()
    v_swap.wait_send()

    @pl.when(core == 0)
    def _():
        u_to_one.wait_send()

    @pl.when(core == 1)
    def _():
        u_to_zero.wait_send()

    @pl.when(slope_to)
    def _():
        slope_back.wait_send()

    @pl.when(ahead_to)
    def _():
        x_ahead.wait_send()

    @pl.when(plain_x)
    def _():
        own_x.wait_send()

    @pl.when(plain_d)
    def _():
        own_d.wait_send()

    @pl.when(bridge_after)
    def _():
        seam_x.wait_send()

    @pl.when(bridge_before)
    def _():
        seam_d.wait_send()

    for condition, copies in (
        (above, [straight for straight, _ in x_up]),
        (jnp.logical_and(above, has_after), [across for _, across in x_up]),
        (below, [straight for straight, _ in d_down]),
        (jnp.logical_and(below, has_before), [across for _, across in d_down]),
    ):

        @pl.when(condition)
        def _(copies=copies):
            for copy in copies:
                copy.wait_send()


def solution(mesh):
    S, T = mesh.shape["segment"], mesh.shape["tm"]
    Y = 4
    Z = T // (2 * Y)
    vmem, hbm = pl.BlockSpec(memory_space=pltpu.VMEM), pl.BlockSpec(memory_space=pltpu.HBM)
    cells = (FRAMES_HERE, 3, 16, 128)

    def body(features, score_cot, clip_frames, conv_weights, norm_gains, score_head):
        out, grad, back = pl.pallas_call(
            functools.partial(kernel, S, T, Y, Z),
            out_shape=(
                jax.ShapeDtypeStruct(cells, BF),
                jax.ShapeDtypeStruct((2, 28, 128, 128), BF),
                jax.ShapeDtypeStruct(cells, BF),
            ),
            in_specs=[
                hbm, hbm, hbm, hbm, hbm, hbm,
            ],
            out_specs=(vmem, vmem, vmem),
            scratch_shapes=[
                pltpu.VMEM((2, FRAMES_HERE, 3, 8, 128), BF),
                pltpu.VMEM((2, 3, FRAMES_HERE, 8), F32),
                pltpu.SMEM((2,), jnp.int32),
                pltpu.VMEM((1, 128), F32),
                pltpu.VMEM((1, 128), F32),
                pltpu.VMEM(cells, BF),
                pltpu.VMEM((2, 3456, 128), BF),
                pltpu.VMEM((2, 3456, 128), BF),
                pltpu.VMEM((10, 3, 16, 128), BF),
                pltpu.VMEM((8, 3, 16, 128), BF),
                pltpu.VMEM((6, 3, 16, 128), F32),
                pltpu.VMEM((10, 5, 16, 384), BF),
                pltpu.VMEM((6, 5, 16, 384), BF),
                pltpu.VMEM((6, 5, 16, 384), BF),
                pltpu.VMEM((6, 3, 16, 128), F32),
                pltpu.VMEM((4, 3, 16, 128), BF),
                pltpu.VMEM((10, 3, 16, 128), BF),
                pltpu.VMEM((384, 512), BF),
                pltpu.VMEM((12, 5, 16, 128), BF),
                pltpu.VMEM((2, 3, 16, 128), BF),
                pltpu.VMEM((28, 128, 128), BF),
                pltpu.VMEM((2, 3, 4, GROUP, BAND, 128), BF),
                pltpu.VMEM((2, 3, GROUP, BAND, 128), BF),
                pltpu.VMEM((2, 3, GROUP, BAND, 128), BF),
                pltpu.VMEM((4, 2, GROUP, BAND, 128), BF),
                pltpu.SemaphoreType.DMA((6,)),
                pltpu.SemaphoreType.DMA((SENDS,)),
                pltpu.SemaphoreType.DMA((SENDS,)),
                pltpu.SemaphoreType.REGULAR,
            ],
            compiler_params=pltpu.CompilerParams(
                collective_id=0, has_side_effects=True, vmem_limit_bytes=40 * 1024 * 1024
            ),
            cost_estimate=pl.CostEstimate(flops=10**9, bytes_accessed=6 * 10**6, transcendentals=10**5),
        )(*(
            pltpu.with_memory_space_constraint(array, pltpu.HBM)
            for array in (
                features, jnp.transpose(score_cot, (0, 2, 1, 3)), clip_frames, conv_weights, norm_gains,
                score_head.reshape(1, 128),
            )
        ))

        def split_clips(cells):
            return jnp.transpose(cells.reshape(FRAMES_HERE, 3, 2, 8, 128), (2, 0, 1, 3, 4))[None]

        return split_clips(out), grad[:, :27].reshape(1, 2, 3456, 128), split_clips(back)

    return jax.shard_map(
        body,
        mesh=mesh,
        in_specs=(
            P("dp", "tm", None, None, None),
            P("dp", "tm", None, None),
            P("dp"),
            P("segment", None, None, None),
            P("segment", None),
            P(),
        ),
        out_specs=(
            P("segment", "dp", "tm", None, None, None),
            P("segment", None, None, None),
            P("segment", "dp", "tm", None, None, None),
        ),
        check_vma=False,
    )
```

```python
import functools

import jax
import jax.numpy as jnp
from jax import lax
from jax.experimental import pallas as pl
from jax.experimental.pallas import tpu as pltpu
from jax.sharding import PartitionSpec as P

norm_eps = 1e-06
FRAMES_HERE = 4
GROUP = 7
BAND = 16
SENDS = 112
BF, F32 = jnp.bfloat16, jnp.float32


def column_shifts(values):
    shape = values.shape
    flat = values.reshape(-1, 8, 128)
    column = lax.broadcasted_iota(jnp.int32, flat.shape, 1)
    before = jnp.where(column == 0, 0.0, pltpu.roll(flat, 1, 1))
    after = jnp.where(column == 7, 0.0, pltpu.roll(flat, 7, 1))
    return [before.reshape(shape), values, after.reshape(shape)]


def fill(patch_ref, values, at=0):
    frames = values.shape[0]
    for e, shifted in enumerate(column_shifts(values)):
        patch_ref[at : at + frames, 1:4, :, e * 128 : (e + 1) * 128] = shifted.astype(BF)


def convolve(patch_ref, weights, which, frames, at=0):
    early_ref, late_ref = weights

    def rows(start, count):
        bands = [patch_ref[start : start + count, b : b + 3].reshape(count * 48, 384) for b in range(3)]
        return jnp.concatenate(bands, axis=1)

    early = jnp.dot(rows(at, frames + 1), early_ref[which], preferred_element_type=F32)
    early = early.reshape(frames + 1, 3, 16, 256)
    late = jnp.dot(rows(at + 2, frames), late_ref[which], preferred_element_type=F32)
    return early[:frames, ..., :128] + early[1:, ..., 128:] + late.reshape(frames, 3, 16, 128)


def kernel(
    S, T, Y, Z,
    feat_hbm, score_hbm, clip_hbm, weight_hbm, gain_hbm, head_hbm,
    out_ref, grad_ref, back_ref,
    feat_ref, score_ref, clip_ref, gain_ref, head_ref, own, early, late, early_flip, late_flip, xin, din, slope, patch8, patch6, patchb, hcot, vsend, vbuf, vt, upad, pcot, gsend, r1, s1, r2, zbuf,
    local_sem, send_sem, recv_sem, ready,
):
    seg, t, x = lax.axis_index("segment"), lax.axis_index("tm"), lax.axis_index("dp")
    core = lax.rem(t, 2)
    y = lax.rem(t // 2, Y)
    z = t // (2 * Y)
    frames = FRAMES_HERE

    def time_of(z, y, core):
        return (z * Y + y) * 2 + core

    def to(seg_to, t_to, x_to):
        return {"segment": seg_to, "tm": t_to, "dp": x_to}

    def remote(source, target, send, recv, device):
        return pltpu.make_async_remote_copy(
            src_ref=source, dst_ref=target, send_sem=send_sem.at[send], recv_sem=recv_sem.at[recv],
            device_id=device, device_id_type=pl.DeviceIdType.MESH,
        )

    loads = [
        pltpu.make_async_copy(source, target, local_sem.at[i])
        for i, (source, target) in enumerate((
            (feat_hbm, feat_ref), (gain_hbm, gain_ref),
            (weight_hbm.at[0, :, pl.ds(0, 1152)], early.at[:, :, pl.ds(0, 128)]),
            (weight_hbm.at[0, :, pl.ds(1152, 1152)], early.at[:, :, pl.ds(128, 128)]),
            (weight_hbm.at[0, :, pl.ds(2304, 1152)], late),
            (score_hbm, score_ref), (clip_hbm, clip_ref), (head_hbm, head_ref),
        ))
    ]
    for load in loads:
        load.start()

    weight, flipped = (early, late), (early_flip, late_flip)

    patch8[:, 0] = jnp.zeros_like(patch8[:, 0])
    patch8[:, 4] = jnp.zeros_like(patch8[:, 4])
    patch6[:, 0] = jnp.zeros_like(patch6[:, 0])
    patch6[:, 4] = jnp.zeros_like(patch6[:, 4])
    patchb[:, 0] = jnp.zeros_like(patchb[:, 0])
    patchb[:, 4] = jnp.zeros_like(patchb[:, 4])
    upad[...] = jnp.zeros_like(upad)
    gsend[27] = jnp.zeros_like(gsend[27])
    has_before, has_after = t > 0, t < T - 1
    seam_after = jnp.logical_and(has_after, lax.rem(t, 2 * Y) == 2 * Y - 1)
    seam_before = jnp.logical_and(has_before, lax.rem(t, 2 * Y) == 0)
    bridge_after = jnp.logical_and(seg == S - 1, seam_after)
    bridge_before = jnp.logical_and(seg == 0, seam_before)
    ahead_to = jnp.logical_and(seg == S - 2, has_before)
    ahead_from = jnp.logical_and(seg == S - 1, has_after)
    below, above = seg > 0, seg < S - 1
    before, after = jnp.maximum(t - 1, 0), jnp.minimum(t + 1, T - 1)
    lower, upper = jnp.maximum(seg - 1, 0), jnp.minimum(seg + 1, S - 1)

    @pl.when(jnp.logical_not(has_before))
    def _():
        xin[0:frames] = jnp.zeros_like(xin[0:frames])

    @pl.when(jnp.logical_not(has_after))
    def _():
        din[frames:] = jnp.zeros_like(din[frames:])
        xin[8:10] = jnp.zeros_like(xin[8:10])
        slope[frames:] = jnp.zeros_like(slope[frames:])

    barrier = pltpu.get_barrier_semaphore()
    expected = 8
    for condition, device in (
        (has_before, to(seg, before, x)),
        (has_after, to(seg, after, x)),
        (above, to(upper, t, x)),
        (jnp.logical_and(above, has_after), to(upper, after, x)),
        (below, to(lower, t, x)),
        (jnp.logical_and(below, has_before), to(lower, before, x)),
        (bridge_after, to(0, after, x)),
        (bridge_before, to(S - 1, before, x)),
        (ahead_to, to(S - 1, before, x)),
        (ahead_from, to(S - 2, after, x)),
    ):
        expected = expected + condition.astype(jnp.int32)

        @pl.when(condition)
        def _(device=device):
            pl.semaphore_signal(barrier, 1, device_id=device, device_id_type=pl.DeviceIdType.MESH)

    for device in [
        *(to(seg, t, lax.rem(x + step, 4)) for step in range(1, 4)),
        *(to(seg, time_of(z, lax.rem(y + step, 4), core), x) for step in range(1, 4)),
        *(to(seg, time_of(lax.rem(z + step, 4), y, core), x) for step in (1, 3)),
    ]:
        pl.semaphore_signal(barrier, 1, device_id=device, device_id_type=pl.DeviceIdType.MESH)

    def put_features(target):
        target[...] = jnp.concatenate([feat_ref[0].astype(F32), feat_ref[1].astype(F32)], axis=2).astype(BF)

    def put_seeds(target):
        eye = lax.broadcasted_iota(jnp.int32, (8, 8), 0) == lax.broadcasted_iota(jnp.int32, (8, 8), 1)
        head = head_ref[...]
        for f in range(frames):
            for i in range(3):
                halves = []
                for n in range(2):
                    line = score_ref[n, i, f : f + 1, :]
                    valid = jnp.where(t * frames + f < clip_ref[n], 1.0, 0.0)
                    stood = jnp.sum(jnp.where(eye, jnp.broadcast_to(line, (8, 8)), 0.0), axis=1, keepdims=True)
                    halves.append((stood * valid) * head)
                target[f, i] = jnp.concatenate(halves, axis=0).astype(BF)

    for load in loads:
        load.wait()

    @pl.when(seg == 0)
    def _():
        put_features(xin.at[pl.ds(frames, frames)])

    @pl.when(seg == S - 1)
    def _():
        put_features(own)
        put_seeds(din.at[pl.ds(0, frames)])

    pl.semaphore_wait(barrier, expected)
    pl.semaphore_signal(
        ready, 1, device_id=to(seg, time_of(lax.rem(z + 3, 4), y, core), x), device_id_type=pl.DeviceIdType.MESH
    )

    x_ahead = remote(out_ref.at[pl.ds(0, 2)], xin.at[pl.ds(8, 2)], 110, 110, to(S - 1, before, x))
    own_x = remote(xin.at[pl.ds(frames, frames)], xin.at[pl.ds(0, frames)], 0, 0, to(seg, after, x))
    own_d = remote(din.at[pl.ds(0, frames)], din.at[pl.ds(frames, frames)], 1, 1, to(seg, before, x))
    seam_x = remote(own, xin.at[pl.ds(0, frames)], 0, 0, to(0, after, x))
    seam_d = remote(own, din.at[pl.ds(frames, frames)], 1, 1, to(S - 1, before, x))
    x_up, d_down = [], []
    for h in range(2):
        here, later = pl.ds(2 * h, 2), pl.ds(frames + 2 * h, 2)
        x_up.append((
            remote(out_ref.at[here], xin.at[later], 2 + h, 2 + h, to(upper, t, x)),
            remote(out_ref.at[here], xin.at[here], 4 + h, 4 + h, to(upper, after, x)),
        ))
        d_down.append((
            remote(back_ref.at[here], din.at[here], 6 + h, 6 + h, to(lower, t, x)),
            remote(back_ref.at[here], din.at[later], 8 + h, 8 + h, to(lower, before, x)),
        ))
    slope_back = remote(slope.at[pl.ds(0, 2)], slope.at[pl.ds(4, 2)], 10, 10, to(seg, before, x))
    partner = to(seg, t + 1 - 2 * core, x)
    v_swap = remote(vsend, vbuf.at[pl.ds(6 * core, 4)], 11, 11, partner)
    u_to_one = remote(din.at[pl.ds(0, 4)], upad.at[pl.ds(2, 4), pl.ds(1, 3)], 12, 12, partner)
    u_to_zero = remote(pcot, upad.at[pl.ds(8, 2), pl.ds(1, 3)], 12, 12, partner)
    plain_x = jnp.logical_and(seg == 0, jnp.logical_and(has_after, jnp.logical_not(seam_after)))
    plain_d = jnp.logical_and(seg == S - 1, jnp.logical_and(has_before, jnp.logical_not(seam_before)))

    @pl.when(plain_x)
    def _():
        own_x.start()

    @pl.when(bridge_after)
    def _():
        seam_x.start()

    @pl.when(plain_d)
    def _():
        own_d.start()

    def flip_all():
        first, middle = pl.ds(0, 128), pl.ds(128, 128)
        pairs = (
            (early, first, late_flip, first), (early, middle, early_flip, middle), (late, first, early_flip, first),
        )

        def one(i, carry):
            source = pl.ds(pl.multiple_of(i * 128, 128), 128)
            target = pl.ds(pl.multiple_of((8 - i) * 128, 128), 128)
            for from_ref, from_columns, to_ref, to_columns in pairs:
                for which in range(2):
                    tap = from_ref[which, source, from_columns].astype(F32)
                    to_ref[which, target, to_columns] = tap.T.astype(BF)
            return carry

        lax.fori_loop(0, 9, one, 0)

    @pl.when(below)
    def _():
        flip_all()

    def hidden_back():
        fill(patch8, din[...].astype(F32))
        hcot[...] = convolve(patch8, flipped, 1, 6)

    @pl.when(jnp.logical_and(seg == S - 1, has_after))
    def _():
        own_d.wait_recv()

    @pl.when(seg == S - 1)
    def _():
        hidden_back()

    @pl.when(below)
    def _():
        for straight, _ in x_up:
            straight.wait_recv()

    @pl.when(jnp.logical_and(below, has_before))
    def _():
        for _, across in x_up:
            across.wait_recv()

    @pl.when(jnp.logical_and(seg == 0, has_before))
    def _():
        own_x.wait_recv()

    gain = gain_ref[...]

    def normalize(values):
        wide = values.astype(F32)
        root = lax.rsqrt(jnp.mean(wide * wide, axis=-1, keepdims=True) + norm_eps)
        return (wide * root * gain).astype(BF).astype(F32)

    normed = normalize(xin[0:8])
    fill(patch8, normed)
    pre = convolve(patch8, weight, 0, 6)
    sig = 1.0 / (1.0 + jnp.exp(-pre))
    hidden = (pre * sig).astype(BF).astype(F32)
    slope[0:4] = (sig * (1.0 + pre * (1.0 - sig)))[2:6]

    @pl.when(ahead_from)
    def _():
        x_ahead.wait_recv()

    @pl.when(seg == S - 1)
    def _():
        fill(patch8, normalize(xin[8:10]), 8)
        later = convolve(patch8, weight, 0, 2, 6)
        share = 1.0 / (1.0 + jnp.exp(-later))
        slope[4:6] = share * (1.0 + later * (1.0 - share))

    slope_to, slope_from = jnp.logical_and(above, has_before), jnp.logical_and(above, has_after)

    @pl.when(slope_to)
    def _():
        slope_back.start()

    fill(patch6, hidden)
    vsend[...] = jnp.where(core == 0, hidden[0:4], normed[4:8]).astype(BF)
    vbuf[pl.ds(4 * core, 6)] = jnp.where(core == 0, normed[2:8], hidden).astype(BF)
    v_swap.start()
    def second_half():
        for h in range(2):
            rows = slice(2 * h, 2 * h + 2)
            second = convolve(patch6, weight, 1, 2, 2 * h)
            out_ref[rows] = (xin[4 + 2 * h : 6 + 2 * h].astype(F32) + second).astype(BF)

            @pl.when(jnp.logical_and(above, has_after))
            def _(h=h):
                x_up[h][1].start()

            @pl.when(above)
            def _(h=h):
                x_up[h][0].start()

            if h == 0:

                @pl.when(ahead_to)
                def _():
                    x_ahead.start()

    @pl.when(above)
    def _():
        second_half()

    def stand_up():
        v_swap.wait_recv()
        flat = vbuf[...].astype(F32)
        for e, shifted in enumerate(column_shifts(flat)):
            rows = jnp.concatenate([shifted.reshape(480, 128), jnp.zeros((32, 128), F32)], axis=0)
            vt[e * 128 : (e + 1) * 128, :] = rows.T.astype(BF)

    @pl.when(bridge_before)
    def _():
        put_seeds(own)
        seam_d.start()

    @pl.when(seg == 0)
    def _():
        flip_all()

    @pl.when(above)
    def _():
        stand_up()

    @pl.when(above)
    def _():
        for straight, _ in d_down:
            straight.wait_recv()

    @pl.when(core == 0)
    def _():
        u_to_one.start()

    @pl.when(core == 1)
    def _():
        upad[6:10, 1:4] = din[0:4]

    @pl.when(jnp.logical_and(above, has_after))
    def _():
        for _, across in d_down:
            across.wait_recv()

    @pl.when(above)
    def _():
        hidden_back()

    @pl.when(slope_from)
    def _():
        slope_back.wait_recv()

    pre_cot = (hcot[...] * slope[...]).astype(BF)

    @pl.when(core == 0)
    def _():
        upad[2:8, 1:4] = pre_cot

    @pl.when(core == 1)
    def _():
        pcot[...] = pre_cot[2:4]
        u_to_zero.start()

    fill(patchb, pre_cot.astype(F32))

    def input_back():
        for h in range(2):
            rows = slice(2 * h, 2 * h + 2)
            normed_cot = convolve(patchb, flipped, 0, 2, 2 * h)
            wide = xin[4 + 2 * h : 6 + 2 * h].astype(F32)
            root = lax.rsqrt(jnp.mean(wide * wide, axis=-1, keepdims=True) + norm_eps)
            weighted = normed_cot * gain
            inner = jnp.mean(weighted * wide, axis=-1, keepdims=True)
            back_ref[rows] = (din[rows].astype(F32) + (root * weighted - wide * root * root * root * inner)).astype(BF)

            @pl.when(jnp.logical_and(below, has_before))
            def _(h=h):
                d_down[h][1].start()

            @pl.when(below)
            def _(h=h):
                d_down[h][0].start()

    postponed = jnp.logical_and(seg == 0, core == 1)

    @pl.when(jnp.logical_not(postponed))
    def _():
        input_back()

    @pl.when(seg == S - 1)
    def _():
        second_half()
        stand_up()

    def on_x(step):
        return to(seg, t, lax.rem(x + step, 4))

    def on_y(step):
        return to(seg, time_of(z, lax.rem(y + step, 4), core), x)

    first, other = (x, y), (y, x)
    on_first, on_other = (on_x, on_y), (on_y, on_x)

    def group_at(h, step):
        return pl.ds(lax.rem(first[h] + step, 4) * GROUP, GROUP)

    def band_at(h, step):
        return pl.ds(pl.multiple_of(64 * h + lax.rem(other[h] + step, 4) * BAND, BAND), BAND)

    def piece(h, j, k):
        return grad_ref.at[core, group_at(h, j), band_at(h, k)]

    @pl.when(core == 0)
    def _():
        u_to_zero.wait_recv()

    @pl.when(core == 1)
    def _():
        u_to_one.wait_recv()

    taps = [(a, b) for a in range(3) for b in range(3)]
    for start in range(0, 9, 2):
        columns = []
        for a, b in taps[start : start + 2]:
            rows = upad[2 - a : 12 - a, 2 - b : 5 - b].reshape(480, 128)
            columns.append(jnp.concatenate([rows, jnp.zeros((32, 128), BF)], axis=0))
        part = jnp.dot(vt[...], jnp.concatenate(columns, axis=1), preferred_element_type=F32).astype(BF)
        for n, (a, b) in enumerate(taps[start : start + 2]):
            gsend[9 * a + 3 * b : 9 * a + 3 * b + 3] = part[:, n * 128 : (n + 1) * 128].reshape(3, 128, 128)

    started = []

    def send(source, target, device):
        index = len(started)
        copy = remote(source, target, 13 + index, 13 + index, device)
        copy.start()
        started.append(copy)
        return copy

    scattered = {}
    for k in (1, 2, 3, 0):
        for j in range(1, 4):
            for h in range(2):
                scattered[h, j, k] = send(gsend.at[group_at(h, j), band_at(h, k)], r1.at[h, j - 1, k], on_first[h](j))

    @pl.when(postponed)
    def _():
        input_back()

    banded, total = {}, [None, None]
    for k in (1, 2, 3, 0):
        for h in range(2):
            total[h] = gsend[group_at(h, 0), band_at(h, k)].astype(F32)
            for j in range(1, 4):
                scattered[h, j, k].wait_recv()
                total[h] = total[h] + r1[h, j - 1, k].astype(F32)
            if k > 0:
                s1[h, k - 1] = total[h].astype(BF)
                banded[h, k] = send(s1.at[h, k - 1], r2.at[h, k - 1], on_other[h](k))
    for h in range(2):
        for k in range(1, 4):
            banded[h, k].wait_recv()
            total[h] = total[h] + r2[h, k - 1].astype(F32)
        zbuf[z, h] = total[h].astype(BF)
    pl.semaphore_wait(ready, 1)
    crossed = [
        send(zbuf.at[z], zbuf.at[z], to(seg, time_of(lax.rem(z + k, 4), y, core), x)) for k in (2, 1, 3)
    ]
    for copy in crossed:
        copy.wait_recv()
    for h in range(2):
        summed = zbuf[0, h].astype(F32)
        for k in range(1, 4):
            summed = summed + zbuf[k, h].astype(F32)
        grad_ref[core, group_at(h, 0), band_at(h, 0)] = summed.astype(BF)

    over_other, over_first, over_pair = {}, {}, []
    for k in range(1, 4):
        for h in range(2):
            over_other[h, k] = send(piece(h, 0, 0), piece(h, 0, 0), on_other[h](k))
    for k in range(4):
        for h in range(2):
            if k > 0:
                over_other[h, k].wait_recv()
            held = piece(h, 0, (4 - k) % 4)
            for j in range(1, 4):
                over_first[h, j, k] = send(held, held, on_first[h](j))
            over_pair.append(send(held, held, partner))
    for k in range(4):
        for j in range(1, 4):
            for h in range(2):
                over_first[h, j, k].wait_recv()
                held = piece(h, 4 - j, (4 - k) % 4)
                over_pair.append(send(held, held, partner))
    for copy in over_pair:
        copy.wait_recv()

    for copy in started:
        copy.wait_send()
    v_swap.wait_send()

    @pl.when(core == 0)
    def _():
        u_to_one.wait_send()

    @pl.when(core == 1)
    def _():
        u_to_zero.wait_send()

    @pl.when(slope_to)
    def _():
        slope_back.wait_send()

    @pl.when(ahead_to)
    def _():
        x_ahead.wait_send()

    @pl.when(plain_x)
    def _():
        own_x.wait_send()

    @pl.when(plain_d)
    def _():
        own_d.wait_send()

    @pl.when(bridge_after)
    def _():
        seam_x.wait_send()

    @pl.when(bridge_before)
    def _():
        seam_d.wait_send()

    for condition, copies in (
        (above, [straight for straight, _ in x_up]),
        (jnp.logical_and(above, has_after), [across for _, across in x_up]),
        (below, [straight for straight, _ in d_down]),
        (jnp.logical_and(below, has_before), [across for _, across in d_down]),
    ):

        @pl.when(condition)
        def _(copies=copies):
            for copy in copies:
                copy.wait_send()


def solution(mesh):
    S, T = mesh.shape["segment"], mesh.shape["tm"]
    Y = 4
    Z = T // (2 * Y)
    vmem, hbm = pl.BlockSpec(memory_space=pltpu.VMEM), pl.BlockSpec(memory_space=pltpu.HBM)
    cells = (FRAMES_HERE, 3, 16, 128)

    def body(features, score_cot, clip_frames, conv_weights, norm_gains, score_head):
        out, grad, back = pl.pallas_call(
            functools.partial(kernel, S, T, Y, Z),
            out_shape=(
                jax.ShapeDtypeStruct(cells, BF),
                jax.ShapeDtypeStruct((2, 28, 128, 128), BF),
                jax.ShapeDtypeStruct(cells, BF),
            ),
            in_specs=[
                hbm, hbm, hbm, hbm, hbm, hbm,
            ],
            out_specs=(vmem, vmem, vmem),
            scratch_shapes=[
                pltpu.VMEM((2, FRAMES_HERE, 3, 8, 128), BF),
                pltpu.VMEM((2, 3, FRAMES_HERE, 8), F32),
                pltpu.SMEM((2,), jnp.int32),
                pltpu.VMEM((1, 128), F32),
                pltpu.VMEM((1, 128), F32),
                pltpu.VMEM(cells, BF),
                pltpu.VMEM((2, 1152, 256), BF),
                pltpu.VMEM((2, 1152, 128), BF),
                pltpu.VMEM((2, 1152, 256), BF),
                pltpu.VMEM((2, 1152, 128), BF),
                pltpu.VMEM((10, 3, 16, 128), BF),
                pltpu.VMEM((8, 3, 16, 128), BF),
                pltpu.VMEM((6, 3, 16, 128), F32),
                pltpu.VMEM((10, 5, 16, 384), BF),
                pltpu.VMEM((6, 5, 16, 384), BF),
                pltpu.VMEM((6, 5, 16, 384), BF),
                pltpu.VMEM((6, 3, 16, 128), F32),
                pltpu.VMEM((4, 3, 16, 128), BF),
                pltpu.VMEM((10, 3, 16, 128), BF),
                pltpu.VMEM((384, 512), BF),
                pltpu.VMEM((12, 5, 16, 128), BF),
                pltpu.VMEM((2, 3, 16, 128), BF),
                pltpu.VMEM((28, 128, 128), BF),
                pltpu.VMEM((2, 3, 4, GROUP, BAND, 128), BF),
                pltpu.VMEM((2, 3, GROUP, BAND, 128), BF),
                pltpu.VMEM((2, 3, GROUP, BAND, 128), BF),
                pltpu.VMEM((4, 2, GROUP, BAND, 128), BF),
                pltpu.SemaphoreType.DMA((8,)),
                pltpu.SemaphoreType.DMA((SENDS,)),
                pltpu.SemaphoreType.DMA((SENDS,)),
                pltpu.SemaphoreType.REGULAR,
            ],
            compiler_params=pltpu.CompilerParams(
                collective_id=0, has_side_effects=True, vmem_limit_bytes=40 * 1024 * 1024
            ),
            cost_estimate=pl.CostEstimate(flops=10**9, bytes_accessed=6 * 10**6, transcendentals=10**5),
        )(*(
            pltpu.with_memory_space_constraint(array, pltpu.HBM)
            for array in (
                features, jnp.transpose(score_cot, (0, 2, 1, 3)), clip_frames, conv_weights, norm_gains,
                score_head.reshape(1, 128),
            )
        ))

        def split_clips(cells):
            return jnp.transpose(cells.reshape(FRAMES_HERE, 3, 2, 8, 128), (2, 0, 1, 3, 4))[None]

        return split_clips(out), grad[:, :27].reshape(1, 2, 3456, 128), split_clips(back)

    return jax.shard_map(
        body,
        mesh=mesh,
        in_specs=(
            P("dp", "tm", None, None, None),
            P("dp", "tm", None, None),
            P("dp"),
            P("segment", None, None, None),
            P("segment", None),
            P(),
        ),
        out_specs=(
            P("segment", "dp", "tm", None, None, None),
            P("segment", None, None, None),
            P("segment", "dp", "tm", None, None, None),
        ),
        check_vma=False,
    )
```

```python
import functools

import jax
import jax.numpy as jnp
from jax import lax
from jax.experimental import pallas as pl
from jax.experimental.pallas import tpu as pltpu
from jax.sharding import PartitionSpec as P

norm_eps = 1e-06
FRAMES_HERE = 4
GROUP = 7
BAND = 16
SENDS = 116
BF, F32 = jnp.bfloat16, jnp.float32


def column_shifts(values):
    shape = values.shape
    flat = values.reshape(-1, 8, 128)
    column = lax.broadcasted_iota(jnp.int32, flat.shape, 1)
    before = jnp.where(column == 0, 0.0, pltpu.roll(flat, 1, 1))
    after = jnp.where(column == 7, 0.0, pltpu.roll(flat, 7, 1))
    return [before.reshape(shape), values, after.reshape(shape)]


def fill(patch_ref, values, at=0):
    frames = values.shape[0]
    for e, shifted in enumerate(column_shifts(values)):
        patch_ref[at : at + frames, 1:4, :, e * 128 : (e + 1) * 128] = shifted.astype(BF)


def convolve(patch_ref, weights, which, frames, at=0):
    early_ref, late_ref = weights

    def rows(start, count):
        bands = [patch_ref[start : start + count, b : b + 3].reshape(count * 48, 384) for b in range(3)]
        return jnp.concatenate(bands, axis=1)

    early = jnp.dot(rows(at, frames + 1), early_ref[which], preferred_element_type=F32)
    early = early.reshape(frames + 1, 3, 16, 256)
    late = jnp.dot(rows(at + 2, frames), late_ref[which], preferred_element_type=F32)
    return early[:frames, ..., :128] + early[1:, ..., 128:] + late.reshape(frames, 3, 16, 128)


def kernel(
    S, T, Y, Z,
    feat_hbm, score_hbm, clip_hbm, weight_hbm, gain_hbm, head_hbm,
    out_ref, grad_ref, back_ref,
    feat_ref, score_ref, clip_ref, gain_ref, head_ref, own, early, late, early_flip, late_flip, xin, din, slope, patch8, patch6, patchb, hcot, roots, vsend, vbuf, vt, upad, pcot, gsend, r1, s1, r2, zbuf,
    local_sem, send_sem, recv_sem, ready,
):
    seg, t, x = lax.axis_index("segment"), lax.axis_index("tm"), lax.axis_index("dp")
    core = lax.rem(t, 2)
    y = lax.rem(t // 2, Y)
    z = t // (2 * Y)
    frames = FRAMES_HERE

    def time_of(z, y, core):
        return (z * Y + y) * 2 + core

    def to(seg_to, t_to, x_to):
        return {"segment": seg_to, "tm": t_to, "dp": x_to}

    def remote(source, target, send, recv, device):
        return pltpu.make_async_remote_copy(
            src_ref=source, dst_ref=target, send_sem=send_sem.at[send], recv_sem=recv_sem.at[recv],
            device_id=device, device_id_type=pl.DeviceIdType.MESH,
        )

    loads = [
        pltpu.make_async_copy(source, target, local_sem.at[i])
        for i, (source, target) in enumerate((
            (feat_hbm, feat_ref), (score_hbm, score_ref), (clip_hbm, clip_ref), (head_hbm, head_ref),
            (gain_hbm, gain_ref),
            (weight_hbm.at[0, :, pl.ds(0, 1152)], early.at[:, :, pl.ds(0, 128)]),
            (weight_hbm.at[0, :, pl.ds(1152, 1152)], early.at[:, :, pl.ds(128, 128)]),
            (weight_hbm.at[0, :, pl.ds(2304, 1152)], late),
        ))
    ]
    for load in loads:
        load.start()

    weight, flipped = (early, late), (early_flip, late_flip)

    has_before, has_after = t > 0, t < T - 1
    seam_after = jnp.logical_and(has_after, lax.rem(t, 2 * Y) == 2 * Y - 1)
    seam_before = jnp.logical_and(has_before, lax.rem(t, 2 * Y) == 0)
    bridge_after = jnp.logical_and(seg == S - 1, seam_after)
    bridge_before = jnp.logical_and(seg == 0, seam_before)
    ahead_to = jnp.logical_and(seg == S - 2, has_before)
    ahead_from = jnp.logical_and(seg == S - 1, has_after)
    below, above = seg > 0, seg < S - 1
    before, after = jnp.maximum(t - 1, 0), jnp.minimum(t + 1, T - 1)
    lower, upper = jnp.maximum(seg - 1, 0), jnp.minimum(seg + 1, S - 1)

    barrier = pltpu.get_barrier_semaphore()
    expected = 8
    for condition, device in (
        (has_before, to(seg, before, x)),
        (has_after, to(seg, after, x)),
        (above, to(upper, t, x)),
        (jnp.logical_and(above, has_after), to(upper, after, x)),
        (below, to(lower, t, x)),
        (jnp.logical_and(below, has_before), to(lower, before, x)),
        (bridge_after, to(0, after, x)),
        (bridge_before, to(S - 1, before, x)),
        (ahead_to, to(S - 1, before, x)),
        (ahead_from, to(S - 2, after, x)),
    ):
        expected = expected + condition.astype(jnp.int32)

        @pl.when(condition)
        def _(device=device):
            pl.semaphore_signal(barrier, 1, device_id=device, device_id_type=pl.DeviceIdType.MESH)

    for device in [
        *(to(seg, t, lax.rem(x + step, 4)) for step in range(1, 4)),
        *(to(seg, time_of(z, lax.rem(y + step, 4), core), x) for step in range(1, 4)),
        *(to(seg, time_of(lax.rem(z + step, 4), y, core), x) for step in (1, 3)),
    ]:
        pl.semaphore_signal(barrier, 1, device_id=device, device_id_type=pl.DeviceIdType.MESH)

    patch8[:, 0] = jnp.zeros_like(patch8[:, 0])
    patch8[:, 4] = jnp.zeros_like(patch8[:, 4])
    patch6[:, 0] = jnp.zeros_like(patch6[:, 0])
    patch6[:, 4] = jnp.zeros_like(patch6[:, 4])
    patchb[:, 0] = jnp.zeros_like(patchb[:, 0])
    patchb[:, 4] = jnp.zeros_like(patchb[:, 4])
    upad[:, 0] = jnp.zeros_like(upad[:, 0])
    upad[:, 4] = jnp.zeros_like(upad[:, 4])
    upad[0:2, 1:4] = jnp.zeros_like(upad[0:2, 1:4])
    upad[10:12, 1:4] = jnp.zeros_like(upad[10:12, 1:4])
    gsend[27] = jnp.zeros_like(gsend[27])
    @pl.when(jnp.logical_not(has_before))
    def _():
        xin[0:frames] = jnp.zeros_like(xin[0:frames])

    @pl.when(jnp.logical_not(has_after))
    def _():
        din[frames:] = jnp.zeros_like(din[frames:])
        xin[8:10] = jnp.zeros_like(xin[8:10])
        slope[frames:] = jnp.zeros_like(slope[frames:])

    def put_features(target):
        target[...] = jnp.concatenate([feat_ref[0].astype(F32), feat_ref[1].astype(F32)], axis=2).astype(BF)

    def put_seeds(target):
        eye = lax.broadcasted_iota(jnp.int32, (8, 8), 0) == lax.broadcasted_iota(jnp.int32, (8, 8), 1)
        head = head_ref[...]
        for f in range(frames):
            for i in range(3):
                halves = []
                for n in range(2):
                    line = score_ref[n, i, f : f + 1, :]
                    valid = jnp.where(t * frames + f < clip_ref[n], 1.0, 0.0)
                    stood = jnp.sum(jnp.where(eye, jnp.broadcast_to(line, (8, 8)), 0.0), axis=1, keepdims=True)
                    halves.append((stood * valid) * head)
                target[f, i] = jnp.concatenate(halves, axis=0).astype(BF)

    for load in loads[:5]:
        load.wait()

    @pl.when(seg == 0)
    def _():
        put_features(xin.at[pl.ds(frames, frames)])

    @pl.when(seg == S - 1)
    def _():
        put_features(own)
        put_seeds(din.at[pl.ds(0, frames)])

    pl.semaphore_wait(barrier, expected)
    pl.semaphore_signal(
        ready, 1, device_id=to(seg, time_of(lax.rem(z + 3, 4), y, core), x), device_id_type=pl.DeviceIdType.MESH
    )

    x_ahead = remote(out_ref.at[pl.ds(0, 2)], xin.at[pl.ds(8, 2)], 115, 115, to(S - 1, before, x))
    own_x = remote(xin.at[pl.ds(frames, frames)], xin.at[pl.ds(0, frames)], 0, 0, to(seg, after, x))
    own_d = remote(din.at[pl.ds(0, frames)], din.at[pl.ds(frames, frames)], 1, 1, to(seg, before, x))
    seam_x = remote(own, xin.at[pl.ds(0, frames)], 0, 0, to(0, after, x))
    seam_d = remote(own, din.at[pl.ds(frames, frames)], 1, 1, to(S - 1, before, x))
    x_up, d_down = [], []
    for h in range(2):
        here, later = pl.ds(2 * h, 2), pl.ds(frames + 2 * h, 2)
        x_up.append((
            remote(out_ref.at[here], xin.at[later], 2 + h, 2 + h, to(upper, t, x)),
            remote(out_ref.at[here], xin.at[here], 4 + h, 4 + h, to(upper, after, x)),
        ))
        d_down.append((
            remote(back_ref.at[here], din.at[here], 6 + h, 6 + h, to(lower, t, x)),
            remote(back_ref.at[here], din.at[later], 8 + h, 8 + h, to(lower, before, x)),
        ))
    slope_back = remote(slope.at[pl.ds(0, 2)], slope.at[pl.ds(4, 2)], 10, 10, to(seg, before, x))
    partner = to(seg, t + 1 - 2 * core, x)
    v_swap = remote(vsend, vbuf.at[pl.ds(6 * core, 4)], 11, 11, partner)
    u_to_one = remote(din.at[pl.ds(0, 4)], upad.at[pl.ds(2, 4), pl.ds(1, 3)], 12, 12, partner)
    u_to_zero = remote(pcot, upad.at[pl.ds(8, 2), pl.ds(1, 3)], 12, 12, partner)
    plain_x = jnp.logical_and(seg == 0, jnp.logical_and(has_after, jnp.logical_not(seam_after)))
    plain_d = jnp.logical_and(seg == S - 1, jnp.logical_and(has_before, jnp.logical_not(seam_before)))

    @pl.when(plain_x)
    def _():
        own_x.start()

    @pl.when(bridge_after)
    def _():
        seam_x.start()

    @pl.when(plain_d)
    def _():
        own_d.start()

    for load in loads[5:]:
        load.wait()

    def flip_all():
        first, middle = pl.ds(0, 128), pl.ds(128, 128)
        pairs = (
            (early, first, late_flip, first), (early, middle, early_flip, middle), (late, first, early_flip, first),
        )

        def one(i, carry):
            source = pl.ds(pl.multiple_of(i * 128, 128), 128)
            target = pl.ds(pl.multiple_of((8 - i) * 128, 128), 128)
            for from_ref, from_columns, to_ref, to_columns in pairs:
                for which in range(2):
                    tap = from_ref[which, source, from_columns].astype(F32)
                    to_ref[which, target, to_columns] = tap.T.astype(BF)
            return carry

        lax.fori_loop(0, 9, one, 0)

    @pl.when(below)
    def _():
        flip_all()

    def hidden_back():
        fill(patch8, din[...].astype(F32))
        hcot[...] = convolve(patch8, flipped, 1, 6)

    @pl.when(jnp.logical_and(seg == S - 1, has_after))
    def _():
        own_d.wait_recv()

    @pl.when(seg == S - 1)
    def _():
        hidden_back()

    @pl.when(below)
    def _():
        for straight, _ in x_up:
            straight.wait_recv()

    @pl.when(jnp.logical_and(below, has_before))
    def _():
        for _, across in x_up:
            across.wait_recv()

    @pl.when(jnp.logical_and(seg == 0, has_before))
    def _():
        own_x.wait_recv()

    gain = gain_ref[...]

    def normalize(values):
        wide = values.astype(F32)
        root = lax.rsqrt(jnp.mean(wide * wide, axis=-1, keepdims=True) + norm_eps)
        return (wide * root * gain).astype(BF).astype(F32), root

    normed, root = normalize(xin[0:8])
    roots[...] = jnp.broadcast_to(root[4:8], roots.shape)
    fill(patch8, normed)
    pre = convolve(patch8, weight, 0, 6)
    sig = 1.0 / (1.0 + jnp.exp(-pre))
    hidden = (pre * sig).astype(BF).astype(F32)
    slope[0:4] = (sig * (1.0 + pre * (1.0 - sig)))[2:6]

    @pl.when(ahead_from)
    def _():
        x_ahead.wait_recv()

    @pl.when(seg == S - 1)
    def _():
        fill(patch8, normalize(xin[8:10])[0], 8)
        later = convolve(patch8, weight, 0, 2, 6)
        share = 1.0 / (1.0 + jnp.exp(-later))
        slope[4:6] = share * (1.0 + later * (1.0 - share))

    slope_to, slope_from = jnp.logical_and(above, has_before), jnp.logical_and(above, has_after)

    @pl.when(slope_to)
    def _():
        slope_back.start()

    fill(patch6, hidden)
    vsend[...] = jnp.where(core == 0, hidden[0:4], normed[4:8]).astype(BF)
    vbuf[pl.ds(4 * core, 6)] = jnp.where(core == 0, normed[2:8], hidden).astype(BF)
    v_swap.start()
    def second_half():
        for h in range(2):
            rows = slice(2 * h, 2 * h + 2)
            second = convolve(patch6, weight, 1, 2, 2 * h)
            out_ref[rows] = (xin[4 + 2 * h : 6 + 2 * h].astype(F32) + second).astype(BF)

            @pl.when(jnp.logical_and(above, has_after))
            def _(h=h):
                x_up[h][1].start()

            @pl.when(above)
            def _(h=h):
                x_up[h][0].start()

            if h == 0:

                @pl.when(ahead_to)
                def _():
                    x_ahead.start()

    @pl.when(above)
    def _():
        second_half()

    def stand_up():
        v_swap.wait_recv()
        flat = vbuf[...].astype(F32)
        for e, shifted in enumerate(column_shifts(flat)):
            rows = jnp.concatenate([shifted.reshape(480, 128), jnp.zeros((32, 128), F32)], axis=0)
            vt[e * 128 : (e + 1) * 128, :] = rows.T.astype(BF)

    @pl.when(bridge_before)
    def _():
        put_seeds(own)
        seam_d.start()

    @pl.when(seg == 0)
    def _():
        flip_all()

    @pl.when(above)
    def _():
        stand_up()

    @pl.when(above)
    def _():
        for straight, _ in d_down:
            straight.wait_recv()

    @pl.when(core == 0)
    def _():
        u_to_one.start()

    @pl.when(core == 1)
    def _():
        upad[6:10, 1:4] = din[0:4]

    @pl.when(jnp.logical_and(above, has_after))
    def _():
        for _, across in d_down:
            across.wait_recv()

    @pl.when(above)
    def _():
        hidden_back()

    @pl.when(slope_from)
    def _():
        slope_back.wait_recv()

    pre_cot = (hcot[...] * slope[...]).astype(BF)

    @pl.when(core == 0)
    def _():
        upad[2:8, 1:4] = pre_cot

    @pl.when(core == 1)
    def _():
        pcot[...] = pre_cot[2:4]
        u_to_zero.start()

    fill(patchb, pre_cot.astype(F32))

    def input_back():
        for h in range(2):
            rows = slice(2 * h, 2 * h + 2)
            normed_cot = convolve(patchb, flipped, 0, 2, 2 * h)
            wide = xin[4 + 2 * h : 6 + 2 * h].astype(F32)
            root = roots[rows]
            weighted = normed_cot * gain
            inner = jnp.mean(weighted * wide, axis=-1, keepdims=True)
            back_ref[rows] = (din[rows].astype(F32) + (root * weighted - wide * root * root * root * inner)).astype(BF)

            @pl.when(jnp.logical_and(below, has_before))
            def _(h=h):
                d_down[h][1].start()

            @pl.when(below)
            def _(h=h):
                d_down[h][0].start()

    postponed = jnp.logical_and(seg == 0, core == 1)

    @pl.when(jnp.logical_not(postponed))
    def _():
        input_back()

    @pl.when(seg == S - 1)
    def _():
        second_half()
        stand_up()

    def on_x(step):
        return to(seg, t, lax.rem(x + step, 4))

    def on_y(step):
        return to(seg, time_of(z, lax.rem(y + step, 4), core), x)

    first, other = (x, y), (y, x)
    on_first, on_other = (on_x, on_y), (on_y, on_x)

    def group_at(h, step):
        return pl.ds(lax.rem(first[h] + step, 4) * GROUP, GROUP)

    def band_at(h, step):
        return pl.ds(pl.multiple_of(64 * h + lax.rem(other[h] + step, 4) * BAND, BAND), BAND)

    def piece(h, j, k):
        return grad_ref.at[core, group_at(h, j), band_at(h, k)]

    @pl.when(core == 0)
    def _():
        u_to_zero.wait_recv()

    @pl.when(core == 1)
    def _():
        u_to_one.wait_recv()

    taps = [(a, b) for a in range(3) for b in range(3)]
    for start in range(0, 9, 2):
        columns = []
        for a, b in taps[start : start + 2]:
            rows = upad[2 - a : 12 - a, 2 - b : 5 - b].reshape(480, 128)
            columns.append(jnp.concatenate([rows, jnp.zeros((32, 128), BF)], axis=0))
        part = jnp.dot(vt[...], jnp.concatenate(columns, axis=1), preferred_element_type=F32).astype(BF)
        for n, (a, b) in enumerate(taps[start : start + 2]):
            gsend[9 * a + 3 * b : 9 * a + 3 * b + 3] = part[:, n * 128 : (n + 1) * 128].reshape(3, 128, 128)

    started = []

    def send(source, target, device):
        index = len(started)
        copy = remote(source, target, 13 + index, 13 + index, device)
        copy.start()
        started.append(copy)
        return copy

    scattered = {}
    for k in (1, 2, 3, 0):
        for j in range(1, 4):
            for h in range(2):
                scattered[h, j, k] = send(gsend.at[group_at(h, j), band_at(h, k)], r1.at[h, j - 1, k], on_first[h](j))

    @pl.when(postponed)
    def _():
        input_back()

    banded, total = {}, [None, None]
    for k in (1, 2, 3, 0):
        for h in range(2):
            total[h] = gsend[group_at(h, 0), band_at(h, k)].astype(F32)
            for j in range(1, 4):
                scattered[h, j, k].wait_recv()
                total[h] = total[h] + r1[h, j - 1, k].astype(F32)
            if k > 0:
                s1[h, k - 1] = total[h].astype(BF)
                banded[h, k] = send(s1.at[h, k - 1], r2.at[h, k - 1], on_other[h](k))
    crossed = []
    for h in range(2):
        for k in range(1, 4):
            banded[h, k].wait_recv()
            total[h] = total[h] + r2[h, k - 1].astype(F32)
        zbuf[z, h] = total[h].astype(BF)
        for k in (2, 1, 3):
            if h == 0 and k == 2:
                pl.semaphore_wait(ready, 1)
            crossed.append(send(zbuf.at[z, h], zbuf.at[z, h], to(seg, time_of(lax.rem(z + k, 4), y, core), x)))
    v_swap.wait_send()

    @pl.when(core == 0)
    def _():
        u_to_one.wait_send()

    @pl.when(core == 1)
    def _():
        u_to_zero.wait_send()

    @pl.when(slope_to)
    def _():
        slope_back.wait_send()

    @pl.when(ahead_to)
    def _():
        x_ahead.wait_send()

    @pl.when(plain_x)
    def _():
        own_x.wait_send()

    @pl.when(plain_d)
    def _():
        own_d.wait_send()

    @pl.when(bridge_after)
    def _():
        seam_x.wait_send()

    @pl.when(bridge_before)
    def _():
        seam_d.wait_send()

    for condition, copies in (
        (above, [straight for straight, _ in x_up]),
        (jnp.logical_and(above, has_after), [across for _, across in x_up]),
        (below, [straight for straight, _ in d_down]),
        (jnp.logical_and(below, has_before), [across for _, across in d_down]),
    ):

        @pl.when(condition)
        def _(copies=copies):
            for copy in copies:
                copy.wait_send()
    for copy in started:
        copy.wait_send()
    for copy in crossed:
        copy.wait_recv()
    for h in range(2):
        summed = zbuf[0, h].astype(F32)
        for k in range(1, 4):
            summed = summed + zbuf[k, h].astype(F32)
        grad_ref[core, group_at(h, 0), band_at(h, 0)] = summed.astype(BF)

    over_other, over_first, over_pair = {}, {}, []
    for k in range(1, 4):
        for h in range(2):
            over_other[h, k] = send(piece(h, 0, 0), piece(h, 0, 0), on_other[h](k))
    for k in range(4):
        for h in range(2):
            if k > 0:
                over_other[h, k].wait_recv()
            held = piece(h, 0, (4 - k) % 4)
            for j in range(1, 4):
                over_first[h, j, k] = send(held, held, on_first[h](j))
            over_pair.append(send(held, held, partner))
    for k in range(4):
        for j in range(1, 4):
            for h in range(2):
                over_first[h, j, k].wait_recv()
                held = piece(h, 4 - j, (4 - k) % 4)
                over_pair.append(send(held, held, partner))
    for copy in [*over_other.values(), *over_first.values()]:
        copy.wait_send()
    for copy in over_pair:
        copy.wait_recv()

    for copy in over_pair:
        copy.wait_send()


def solution(mesh):
    S, T = mesh.shape["segment"], mesh.shape["tm"]
    Y = 4
    Z = T // (2 * Y)
    vmem, hbm = pl.BlockSpec(memory_space=pltpu.VMEM), pl.BlockSpec(memory_space=pltpu.HBM)
    cells = (FRAMES_HERE, 3, 16, 128)

    def body(features, score_cot, clip_frames, conv_weights, norm_gains, score_head):
        out, grad, back = pl.pallas_call(
            functools.partial(kernel, S, T, Y, Z),
            out_shape=(
                jax.ShapeDtypeStruct(cells, BF),
                jax.ShapeDtypeStruct((2, 28, 128, 128), BF),
                jax.ShapeDtypeStruct(cells, BF),
            ),
            in_specs=[
                hbm, hbm, hbm, hbm, hbm, hbm,
            ],
            out_specs=(vmem, vmem, vmem),
            scratch_shapes=[
                pltpu.VMEM((2, FRAMES_HERE, 3, 8, 128), BF),
                pltpu.VMEM((2, 3, FRAMES_HERE, 8), F32),
                pltpu.SMEM((2,), jnp.int32),
                pltpu.VMEM((1, 128), F32),
                pltpu.VMEM((1, 128), F32),
                pltpu.VMEM(cells, BF),
                pltpu.VMEM((2, 1152, 256), BF),
                pltpu.VMEM((2, 1152, 128), BF),
                pltpu.VMEM((2, 1152, 256), BF),
                pltpu.VMEM((2, 1152, 128), BF),
                pltpu.VMEM((10, 3, 16, 128), BF),
                pltpu.VMEM((8, 3, 16, 128), BF),
                pltpu.VMEM((6, 3, 16, 128), F32),
                pltpu.VMEM((10, 5, 16, 384), BF),
                pltpu.VMEM((6, 5, 16, 384), BF),
                pltpu.VMEM((6, 5, 16, 384), BF),
                pltpu.VMEM((6, 3, 16, 128), F32),
                pltpu.VMEM(cells, F32),
                pltpu.VMEM((4, 3, 16, 128), BF),
                pltpu.VMEM((10, 3, 16, 128), BF),
                pltpu.VMEM((384, 512), BF),
                pltpu.VMEM((12, 5, 16, 128), BF),
                pltpu.VMEM((2, 3, 16, 128), BF),
                pltpu.VMEM((28, 128, 128), BF),
                pltpu.VMEM((2, 3, 4, GROUP, BAND, 128), BF),
                pltpu.VMEM((2, 3, GROUP, BAND, 128), BF),
                pltpu.VMEM((2, 3, GROUP, BAND, 128), BF),
                pltpu.VMEM((4, 2, GROUP, BAND, 128), BF),
                pltpu.SemaphoreType.DMA((8,)),
                pltpu.SemaphoreType.DMA((SENDS,)),
                pltpu.SemaphoreType.DMA((SENDS,)),
                pltpu.SemaphoreType.REGULAR,
            ],
            compiler_params=pltpu.CompilerParams(
                collective_id=0, has_side_effects=True, vmem_limit_bytes=40 * 1024 * 1024
            ),
            cost_estimate=pl.CostEstimate(flops=10**9, bytes_accessed=6 * 10**6, transcendentals=10**5),
        )(*(
            pltpu.with_memory_space_constraint(array, pltpu.HBM)
            for array in (
                features, jnp.transpose(score_cot, (0, 2, 1, 3)), clip_frames, conv_weights, norm_gains,
                score_head.reshape(1, 128),
            )
        ))

        def split_clips(cells):
            return jnp.transpose(cells.reshape(FRAMES_HERE, 3, 2, 8, 128), (2, 0, 1, 3, 4))[None]

        return split_clips(out), grad[:, :27].reshape(1, 2, 3456, 128), split_clips(back)

    return jax.shard_map(
        body,
        mesh=mesh,
        in_specs=(
            P("dp", "tm", None, None, None),
            P("dp", "tm", None, None),
            P("dp"),
            P("segment", None, None, None),
            P("segment", None),
            P(),
        ),
        out_specs=(
            P("segment", "dp", "tm", None, None, None),
            P("segment", None, None, None),
            P("segment", "dp", "tm", None, None, None),
        ),
        check_vma=False,
    )
```

```python
import functools

import jax
import jax.numpy as jnp
from jax import lax
from jax.experimental import pallas as pl
from jax.experimental.pallas import tpu as pltpu
from jax.sharding import PartitionSpec as P

norm_eps = 1e-06
FRAMES_HERE = 4
GROUP = 7
BAND = 16
SENDS = 116
BF, F32 = jnp.bfloat16, jnp.float32


def column_shifts(values):
    shape = values.shape
    flat = values.reshape(-1, 8, 128)
    column = lax.broadcasted_iota(jnp.int32, flat.shape, 1)
    before = jnp.where(column == 0, 0.0, pltpu.roll(flat, 1, 1))
    after = jnp.where(column == 7, 0.0, pltpu.roll(flat, 7, 1))
    return [before.reshape(shape), values, after.reshape(shape)]


def fill(patch_ref, values, at=0):
    frames = values.shape[0]
    for e, shifted in enumerate(column_shifts(values)):
        patch_ref[at : at + frames, 1:4, :, e * 128 : (e + 1) * 128] = shifted.astype(BF)


def convolve(patch_ref, weights, which, frames, at=0):
    early_ref, late_ref = weights

    def rows(start, count):
        bands = [patch_ref[start : start + count, b : b + 3].reshape(count * 48, 384) for b in range(3)]
        return jnp.concatenate(bands, axis=1)

    early = jnp.dot(rows(at, frames + 1), early_ref[which], preferred_element_type=F32)
    early = early.reshape(frames + 1, 3, 16, 256)
    late = jnp.dot(rows(at + 2, frames), late_ref[which], preferred_element_type=F32)
    return early[:frames, ..., :128] + early[1:, ..., 128:] + late.reshape(frames, 3, 16, 128)


def kernel(
    S, T, Y, Z,
    feat_hbm, score_hbm, clip_hbm, weight_hbm, gain_hbm, head_hbm,
    out_ref, grad_ref, back_ref,
    feat_ref, score_ref, clip_ref, gain_ref, head_ref, own, early, late, early_flip, late_flip, xin, din, slope, patch8, patch6, patchb, hcot, roots, vsend, vbuf, vt, upad, pcot, gsend, r1, s1, r2, zbuf,
    local_sem, send_sem, recv_sem, ready,
):
    seg, t, x = lax.axis_index("segment"), lax.axis_index("tm"), lax.axis_index("dp")
    core = lax.rem(t, 2)
    y = lax.rem(t // 2, Y)
    z = t // (2 * Y)
    frames = FRAMES_HERE

    def time_of(z, y, core):
        return (z * Y + y) * 2 + core

    def to(seg_to, t_to, x_to):
        return {"segment": seg_to, "tm": t_to, "dp": x_to}

    def remote(source, target, send, recv, device):
        return pltpu.make_async_remote_copy(
            src_ref=source, dst_ref=target, send_sem=send_sem.at[send], recv_sem=recv_sem.at[recv],
            device_id=device, device_id_type=pl.DeviceIdType.MESH,
        )

    loads = [
        pltpu.make_async_copy(source, target, local_sem.at[i])
        for i, (source, target) in enumerate((
            (feat_hbm, feat_ref), (score_hbm, score_ref), (clip_hbm, clip_ref), (head_hbm, head_ref),
            (gain_hbm, gain_ref),
            (weight_hbm.at[0, :, pl.ds(0, 1152)], early.at[:, :, pl.ds(0, 128)]),
            (weight_hbm.at[0, :, pl.ds(1152, 1152)], early.at[:, :, pl.ds(128, 128)]),
            (weight_hbm.at[0, :, pl.ds(2304, 1152)], late),
        ))
    ]
    for load in loads:
        load.start()

    weight, flipped = (early, late), (early_flip, late_flip)

    has_before, has_after = t > 0, t < T - 1
    seam_after = jnp.logical_and(has_after, lax.rem(t, 2 * Y) == 2 * Y - 1)
    seam_before = jnp.logical_and(has_before, lax.rem(t, 2 * Y) == 0)
    bridge_after = jnp.logical_and(seg == S - 1, seam_after)
    bridge_before = jnp.logical_and(seg == 0, seam_before)
    ahead_to = jnp.logical_and(seg == S - 2, has_before)
    ahead_from = jnp.logical_and(seg == S - 1, has_after)
    below, above = seg > 0, seg < S - 1
    before, after = jnp.maximum(t - 1, 0), jnp.minimum(t + 1, T - 1)
    lower, upper = jnp.maximum(seg - 1, 0), jnp.minimum(seg + 1, S - 1)

    barrier = pltpu.get_barrier_semaphore()
    expected = 8
    for condition, device in (
        (has_before, to(seg, before, x)),
        (has_after, to(seg, after, x)),
        (above, to(upper, t, x)),
        (jnp.logical_and(above, has_after), to(upper, after, x)),
        (below, to(lower, t, x)),
        (jnp.logical_and(below, has_before), to(lower, before, x)),
        (bridge_after, to(0, after, x)),
        (bridge_before, to(S - 1, before, x)),
        (ahead_to, to(S - 1, before, x)),
        (ahead_from, to(S - 2, after, x)),
    ):
        expected = expected + condition.astype(jnp.int32)

        @pl.when(condition)
        def _(device=device):
            pl.semaphore_signal(barrier, 1, device_id=device, device_id_type=pl.DeviceIdType.MESH)

    for device in [
        *(to(seg, t, lax.rem(x + step, 4)) for step in range(1, 4)),
        *(to(seg, time_of(z, lax.rem(y + step, 4), core), x) for step in range(1, 4)),
        *(to(seg, time_of(lax.rem(z + step, 4), y, core), x) for step in (1, 3)),
    ]:
        pl.semaphore_signal(barrier, 1, device_id=device, device_id_type=pl.DeviceIdType.MESH)

    patch8[:, 0] = jnp.zeros_like(patch8[:, 0])
    patch8[:, 4] = jnp.zeros_like(patch8[:, 4])
    patch6[:, 0] = jnp.zeros_like(patch6[:, 0])
    patch6[:, 4] = jnp.zeros_like(patch6[:, 4])
    patchb[:, 0] = jnp.zeros_like(patchb[:, 0])
    patchb[:, 4] = jnp.zeros_like(patchb[:, 4])
    upad[:, 0] = jnp.zeros_like(upad[:, 0])
    upad[:, 4] = jnp.zeros_like(upad[:, 4])
    upad[0:2, 1:4] = jnp.zeros_like(upad[0:2, 1:4])
    upad[10:12, 1:4] = jnp.zeros_like(upad[10:12, 1:4])
    gsend[27] = jnp.zeros_like(gsend[27])
    @pl.when(jnp.logical_not(has_before))
    def _():
        xin[0:frames] = jnp.zeros_like(xin[0:frames])

    @pl.when(jnp.logical_not(has_after))
    def _():
        din[frames:] = jnp.zeros_like(din[frames:])
        xin[8:10] = jnp.zeros_like(xin[8:10])
        slope[frames:] = jnp.zeros_like(slope[frames:])

    def put_features(target):
        target[...] = jnp.concatenate([feat_ref[0].astype(F32), feat_ref[1].astype(F32)], axis=2).astype(BF)

    def put_seeds(target):
        eye = lax.broadcasted_iota(jnp.int32, (8, 8), 0) == lax.broadcasted_iota(jnp.int32, (8, 8), 1)
        head = head_ref[...]
        for f in range(frames):
            for i in range(3):
                halves = []
                for n in range(2):
                    line = score_ref[n, i, f : f + 1, :]
                    valid = jnp.where(t * frames + f < clip_ref[n], 1.0, 0.0)
                    stood = jnp.sum(jnp.where(eye, jnp.broadcast_to(line, (8, 8)), 0.0), axis=1, keepdims=True)
                    halves.append((stood * valid) * head)
                target[f, i] = jnp.concatenate(halves, axis=0).astype(BF)

    for load in loads[:5]:
        load.wait()

    @pl.when(seg == 0)
    def _():
        put_features(xin.at[pl.ds(frames, frames)])

    @pl.when(seg == S - 1)
    def _():
        put_features(own)
        put_seeds(din.at[pl.ds(0, frames)])

    pl.semaphore_wait(barrier, expected)
    pl.semaphore_signal(
        ready, 1, device_id=to(seg, time_of(lax.rem(z + 3, 4), y, core), x), device_id_type=pl.DeviceIdType.MESH
    )

    x_ahead = remote(out_ref.at[pl.ds(0, 2)], xin.at[pl.ds(8, 2)], 115, 115, to(S - 1, before, x))
    own_x = remote(xin.at[pl.ds(frames, frames)], xin.at[pl.ds(0, frames)], 0, 0, to(seg, after, x))
    own_d = remote(din.at[pl.ds(0, frames)], din.at[pl.ds(frames, frames)], 1, 1, to(seg, before, x))
    seam_x = remote(own, xin.at[pl.ds(0, frames)], 0, 0, to(0, after, x))
    seam_d = remote(own, din.at[pl.ds(frames, frames)], 1, 1, to(S - 1, before, x))
    x_up, d_down = [], []
    for h in range(2):
        here, later = pl.ds(2 * h, 2), pl.ds(frames + 2 * h, 2)
        x_up.append((
            remote(out_ref.at[here], xin.at[later], 2 + h, 2 + h, to(upper, t, x)),
            remote(out_ref.at[here], xin.at[here], 4 + h, 4 + h, to(upper, after, x)),
        ))
        d_down.append((
            remote(back_ref.at[here], din.at[here], 6 + h, 6 + h, to(lower, t, x)),
            remote(back_ref.at[here], din.at[later], 8 + h, 8 + h, to(lower, before, x)),
        ))
    slope_back = remote(slope.at[pl.ds(0, 2)], slope.at[pl.ds(4, 2)], 10, 10, to(seg, before, x))
    partner = to(seg, t + 1 - 2 * core, x)
    v_swap = remote(vsend, vbuf.at[pl.ds(6 * core, 4)], 11, 11, partner)
    u_to_one = remote(din.at[pl.ds(0, 4)], upad.at[pl.ds(2, 4), pl.ds(1, 3)], 12, 12, partner)
    u_to_zero = remote(pcot, upad.at[pl.ds(8, 2), pl.ds(1, 3)], 12, 12, partner)
    plain_x = jnp.logical_and(seg == 0, jnp.logical_and(has_after, jnp.logical_not(seam_after)))
    plain_d = jnp.logical_and(seg == S - 1, jnp.logical_and(has_before, jnp.logical_not(seam_before)))

    @pl.when(plain_x)
    def _():
        own_x.start()

    @pl.when(bridge_after)
    def _():
        seam_x.start()

    @pl.when(plain_d)
    def _():
        own_d.start()

    for load in loads[5:]:
        load.wait()

    def flip_all():
        first, middle = pl.ds(0, 128), pl.ds(128, 128)
        pairs = (
            (early, first, late_flip, first), (early, middle, early_flip, middle), (late, first, early_flip, first),
        )

        def one(i, carry):
            source = pl.ds(pl.multiple_of(i * 128, 128), 128)
            target = pl.ds(pl.multiple_of((8 - i) * 128, 128), 128)
            for from_ref, from_columns, to_ref, to_columns in pairs:
                for which in range(2):
                    tap = from_ref[which, source, from_columns].astype(F32)
                    to_ref[which, target, to_columns] = tap.T.astype(BF)
            return carry

        lax.fori_loop(0, 9, one, 0)

    @pl.when(below)
    def _():
        flip_all()

    def hidden_back():
        fill(patch8, din[...].astype(F32))
        hcot[...] = convolve(patch8, flipped, 1, 6)

    @pl.when(jnp.logical_and(seg == S - 1, has_after))
    def _():
        own_d.wait_recv()

    @pl.when(seg == S - 1)
    def _():
        hidden_back()

    @pl.when(below)
    def _():
        for straight, _ in x_up:
            straight.wait_recv()

    @pl.when(jnp.logical_and(below, has_before))
    def _():
        for _, across in x_up:
            across.wait_recv()

    @pl.when(jnp.logical_and(seg == 0, has_before))
    def _():
        own_x.wait_recv()

    gain = gain_ref[...]

    def normalize(values):
        wide = values.astype(F32)
        root = lax.rsqrt(jnp.mean(wide * wide, axis=-1, keepdims=True) + norm_eps)
        return (wide * root * gain).astype(BF).astype(F32), root

    normed, root = normalize(xin[0:8])
    roots[...] = jnp.broadcast_to(root[4:8], roots.shape)
    fill(patch8, normed)
    pre = convolve(patch8, weight, 0, 6)
    sig = 1.0 / (1.0 + jnp.exp(-pre))
    hidden = (pre * sig).astype(BF).astype(F32)
    slope[0:4] = (sig * (1.0 + pre * (1.0 - sig)))[2:6]

    @pl.when(ahead_from)
    def _():
        x_ahead.wait_recv()

    @pl.when(seg == S - 1)
    def _():
        fill(patch8, normalize(xin[8:10])[0], 8)
        later = convolve(patch8, weight, 0, 2, 6)
        share = 1.0 / (1.0 + jnp.exp(-later))
        slope[4:6] = share * (1.0 + later * (1.0 - share))

    slope_to, slope_from = jnp.logical_and(above, has_before), jnp.logical_and(above, has_after)

    @pl.when(slope_to)
    def _():
        slope_back.start()

    fill(patch6, hidden)
    vsend[...] = jnp.where(core == 0, hidden[0:4], normed[4:8]).astype(BF)
    vbuf[pl.ds(4 * core, 6)] = jnp.where(core == 0, normed[2:8], hidden).astype(BF)
    v_swap.start()
    def second_half():
        for h in range(2):
            rows = slice(2 * h, 2 * h + 2)
            second = convolve(patch6, weight, 1, 2, 2 * h)
            out_ref[rows] = (xin[4 + 2 * h : 6 + 2 * h].astype(F32) + second).astype(BF)

            @pl.when(jnp.logical_and(above, has_after))
            def _(h=h):
                x_up[h][1].start()

            @pl.when(above)
            def _(h=h):
                x_up[h][0].start()

            if h == 0:

                @pl.when(ahead_to)
                def _():
                    x_ahead.start()

    @pl.when(above)
    def _():
        second_half()

    def stand_up():
        v_swap.wait_recv()
        flat = vbuf[...].astype(F32)
        for e, shifted in enumerate(column_shifts(flat)):
            rows = jnp.concatenate([shifted.reshape(480, 128), jnp.zeros((32, 128), F32)], axis=0)
            vt[e * 128 : (e + 1) * 128, :] = rows.T.astype(BF)

    @pl.when(bridge_before)
    def _():
        put_seeds(own)
        seam_d.start()

    @pl.when(seg == 0)
    def _():
        flip_all()

    @pl.when(above)
    def _():
        stand_up()

    @pl.when(above)
    def _():
        for straight, _ in d_down:
            straight.wait_recv()

    @pl.when(core == 0)
    def _():
        u_to_one.start()

    @pl.when(core == 1)
    def _():
        upad[6:10, 1:4] = din[0:4]

    @pl.when(jnp.logical_and(above, has_after))
    def _():
        for _, across in d_down:
            across.wait_recv()

    @pl.when(above)
    def _():
        hidden_back()

    @pl.when(slope_from)
    def _():
        slope_back.wait_recv()

    pre_cot = (hcot[...] * slope[...]).astype(BF)

    @pl.when(core == 0)
    def _():
        upad[2:8, 1:4] = pre_cot

    @pl.when(core == 1)
    def _():
        pcot[...] = pre_cot[2:4]
        u_to_zero.start()

    fill(patchb, pre_cot.astype(F32))

    def input_back():
        for h in range(2):
            rows = slice(2 * h, 2 * h + 2)
            normed_cot = convolve(patchb, flipped, 0, 2, 2 * h)
            wide = xin[4 + 2 * h : 6 + 2 * h].astype(F32)
            root = roots[rows]
            weighted = normed_cot * gain
            inner = jnp.mean(weighted * wide, axis=-1, keepdims=True)
            back_ref[rows] = (din[rows].astype(F32) + (root * weighted - wide * root * root * root * inner)).astype(BF)

            @pl.when(jnp.logical_and(below, has_before))
            def _(h=h):
                d_down[h][1].start()

            @pl.when(below)
            def _(h=h):
                d_down[h][0].start()

    postponed = jnp.logical_and(seg == 0, core == 1)

    @pl.when(jnp.logical_not(postponed))
    def _():
        input_back()

    @pl.when(seg == S - 1)
    def _():
        second_half()
        stand_up()

    def on_x(step):
        return to(seg, t, lax.rem(x + step, 4))

    def on_y(step):
        return to(seg, time_of(z, lax.rem(y + step, 4), core), x)

    first, other = (x, y), (y, x)
    on_first, on_other = (on_x, on_y), (on_y, on_x)

    def group_at(h, step):
        return pl.ds(lax.rem(first[h] + step, 4) * GROUP, GROUP)

    def band_at(h, step):
        return pl.ds(pl.multiple_of(64 * h + lax.rem(other[h] + step, 4) * BAND, BAND), BAND)

    def piece(h, j, k):
        return grad_ref.at[core, group_at(h, j), band_at(h, k)]

    @pl.when(core == 0)
    def _():
        u_to_zero.wait_recv()

    @pl.when(core == 1)
    def _():
        u_to_one.wait_recv()

    taps = [(a, b) for a in range(3) for b in range(3)]
    for start in range(0, 9, 2):
        columns = []
        for a, b in taps[start : start + 2]:
            rows = upad[2 - a : 12 - a, 2 - b : 5 - b].reshape(480, 128)
            columns.append(jnp.concatenate([rows, jnp.zeros((32, 128), BF)], axis=0))
        part = jnp.dot(vt[...], jnp.concatenate(columns, axis=1), preferred_element_type=F32).astype(BF)
        for n, (a, b) in enumerate(taps[start : start + 2]):
            gsend[9 * a + 3 * b : 9 * a + 3 * b + 3] = part[:, n * 128 : (n + 1) * 128].reshape(3, 128, 128)

    started = []

    def send(source, target, device):
        index = len(started)
        copy = remote(source, target, 13 + index, 13 + index, device)
        copy.start()
        started.append(copy)
        return copy

    scattered = {}
    for k in (1, 2, 3, 0):
        for j in (2, 1, 3):
            for h in range(2):
                scattered[h, j, k] = send(gsend.at[group_at(h, j), band_at(h, k)], r1.at[h, j - 1, k], on_first[h](j))

    @pl.when(postponed)
    def _():
        input_back()

    banded, total = {}, [None, None]
    for k in (1, 2, 3, 0):
        for h in range(2):
            total[h] = gsend[group_at(h, 0), band_at(h, k)].astype(F32)
            for j in range(1, 4):
                scattered[h, j, k].wait_recv()
                total[h] = total[h] + r1[h, j - 1, k].astype(F32)
            if k > 0:
                s1[h, k - 1] = total[h].astype(BF)
                banded[h, k] = send(s1.at[h, k - 1], r2.at[h, k - 1], on_other[h](k))
    crossed = []
    for h in range(2):
        for k in range(1, 4):
            banded[h, k].wait_recv()
            total[h] = total[h] + r2[h, k - 1].astype(F32)
        zbuf[z, h] = total[h].astype(BF)
        for k in (2, 1, 3):
            if h == 0 and k == 2:
                pl.semaphore_wait(ready, 1)
            crossed.append(send(zbuf.at[z, h], zbuf.at[z, h], to(seg, time_of(lax.rem(z + k, 4), y, core), x)))
    v_swap.wait_send()

    @pl.when(core == 0)
    def _():
        u_to_one.wait_send()

    @pl.when(core == 1)
    def _():
        u_to_zero.wait_send()

    @pl.when(slope_to)
    def _():
        slope_back.wait_send()

    @pl.when(ahead_to)
    def _():
        x_ahead.wait_send()

    @pl.when(plain_x)
    def _():
        own_x.wait_send()

    @pl.when(plain_d)
    def _():
        own_d.wait_send()

    @pl.when(bridge_after)
    def _():
        seam_x.wait_send()

    @pl.when(bridge_before)
    def _():
        seam_d.wait_send()

    for condition, copies in (
        (above, [straight for straight, _ in x_up]),
        (jnp.logical_and(above, has_after), [across for _, across in x_up]),
        (below, [straight for straight, _ in d_down]),
        (jnp.logical_and(below, has_before), [across for _, across in d_down]),
    ):

        @pl.when(condition)
        def _(copies=copies):
            for copy in copies:
                copy.wait_send()
    for copy in started:
        copy.wait_send()
    for copy in crossed:
        copy.wait_recv()
    for h in range(2):
        summed = zbuf[0, h].astype(F32)
        for k in range(1, 4):
            summed = summed + zbuf[k, h].astype(F32)
        grad_ref[core, group_at(h, 0), band_at(h, 0)] = summed.astype(BF)

    over_other, over_first, over_pair = {}, {}, []
    for k in (2, 1, 3):
        for h in range(2):
            over_other[h, k] = send(piece(h, 0, 0), piece(h, 0, 0), on_other[h](k))
    for k in range(4):
        for h in range(2):
            if k > 0:
                over_other[h, k].wait_recv()
            held = piece(h, 0, (4 - k) % 4)
            for j in (2, 1, 3):
                over_first[h, j, k] = send(held, held, on_first[h](j))
            over_pair.append(send(held, held, partner))
    for k in range(4):
        for j in range(1, 4):
            for h in range(2):
                over_first[h, j, k].wait_recv()
                held = piece(h, 4 - j, (4 - k) % 4)
                over_pair.append(send(held, held, partner))
    for copy in [*over_other.values(), *over_first.values()]:
        copy.wait_send()
    for copy in over_pair:
        copy.wait_recv()

    for copy in over_pair:
        copy.wait_send()


def solution(mesh):
    S, T = mesh.shape["segment"], mesh.shape["tm"]
    Y = 4
    Z = T // (2 * Y)
    vmem, hbm = pl.BlockSpec(memory_space=pltpu.VMEM), pl.BlockSpec(memory_space=pltpu.HBM)
    cells = (FRAMES_HERE, 3, 16, 128)

    def body(features, score_cot, clip_frames, conv_weights, norm_gains, score_head):
        out, grad, back = pl.pallas_call(
            functools.partial(kernel, S, T, Y, Z),
            out_shape=(
                jax.ShapeDtypeStruct(cells, BF),
                jax.ShapeDtypeStruct((2, 28, 128, 128), BF),
                jax.ShapeDtypeStruct(cells, BF),
            ),
            in_specs=[
                hbm, hbm, hbm, hbm, hbm, hbm,
            ],
            out_specs=(vmem, vmem, vmem),
            scratch_shapes=[
                pltpu.VMEM((2, FRAMES_HERE, 3, 8, 128), BF),
                pltpu.VMEM((2, 3, FRAMES_HERE, 8), F32),
                pltpu.SMEM((2,), jnp.int32),
                pltpu.VMEM((1, 128), F32),
                pltpu.VMEM((1, 128), F32),
                pltpu.VMEM(cells, BF),
                pltpu.VMEM((2, 1152, 256), BF),
                pltpu.VMEM((2, 1152, 128), BF),
                pltpu.VMEM((2, 1152, 256), BF),
                pltpu.VMEM((2, 1152, 128), BF),
                pltpu.VMEM((10, 3, 16, 128), BF),
                pltpu.VMEM((8, 3, 16, 128), BF),
                pltpu.VMEM((6, 3, 16, 128), F32),
                pltpu.VMEM((10, 5, 16, 384), BF),
                pltpu.VMEM((6, 5, 16, 384), BF),
                pltpu.VMEM((6, 5, 16, 384), BF),
                pltpu.VMEM((6, 3, 16, 128), F32),
                pltpu.VMEM(cells, F32),
                pltpu.VMEM((4, 3, 16, 128), BF),
                pltpu.VMEM((10, 3, 16, 128), BF),
                pltpu.VMEM((384, 512), BF),
                pltpu.VMEM((12, 5, 16, 128), BF),
                pltpu.VMEM((2, 3, 16, 128), BF),
                pltpu.VMEM((28, 128, 128), BF),
                pltpu.VMEM((2, 3, 4, GROUP, BAND, 128), BF),
                pltpu.VMEM((2, 3, GROUP, BAND, 128), BF),
                pltpu.VMEM((2, 3, GROUP, BAND, 128), BF),
                pltpu.VMEM((4, 2, GROUP, BAND, 128), BF),
                pltpu.SemaphoreType.DMA((8,)),
                pltpu.SemaphoreType.DMA((SENDS,)),
                pltpu.SemaphoreType.DMA((SENDS,)),
                pltpu.SemaphoreType.REGULAR,
            ],
            compiler_params=pltpu.CompilerParams(
                collective_id=0, has_side_effects=True, vmem_limit_bytes=40 * 1024 * 1024
            ),
            cost_estimate=pl.CostEstimate(flops=10**9, bytes_accessed=6 * 10**6, transcendentals=10**5),
        )(*(
            pltpu.with_memory_space_constraint(array, pltpu.HBM)
            for array in (
                features, jnp.transpose(score_cot, (0, 2, 1, 3)), clip_frames, conv_weights, norm_gains,
                score_head.reshape(1, 128),
            )
        ))

        def split_clips(cells):
            return jnp.transpose(cells.reshape(FRAMES_HERE, 3, 2, 8, 128), (2, 0, 1, 3, 4))[None]

        return split_clips(out), grad[:, :27].reshape(1, 2, 3456, 128), split_clips(back)

    return jax.shard_map(
        body,
        mesh=mesh,
        in_specs=(
            P("dp", "tm", None, None, None),
            P("dp", "tm", None, None),
            P("dp"),
            P("segment", None, None, None),
            P("segment", None),
            P(),
        ),
        out_specs=(
            P("segment", "dp", "tm", None, None, None),
            P("segment", None, None, None),
            P("segment", "dp", "tm", None, None, None),
        ),
        check_vma=False,
    )
```
